32 devices in a mesh: grp: 2 (over y), row: 4 (over z), col: 2 (over core), chan: 2 (over x).
Axes of the slice: x: 2, y: 2, z: 4, core: 2. Of those that a mesh axis runs over, the one named last changes fastest.
Arguments:
- theta: bfloat16 [2048, 16, 1024], P(('grp', 'row'), None, ('col', 'chan')), parts along dimension 0, may hold values from -6 to 6
- left_env: bfloat16 [2048, 12, 1024], P(('grp', 'row')), parts along dimension 0, may hold values from -0.25 to 0.25
- right_env: bfloat16 [2048, 12, 1024], P('grp', None, ('col', 'chan')), parts along dimension 0, may hold values from -0.078125 to 0.078125
- mpo_left: float32 [12, 12, 4, 4], replicated, may hold values from -0.875 to 0.875
- mpo_right: float32 [12, 12, 4, 4], replicated, may hold values from -0.875 to 0.875
Outputs:
- residual: bfloat16 [2048, 16384], P(('grp', 'col', 'chan'), 'row'), parts along dimension 0
- hvp: bfloat16 [2048, 16, 1024], P(('grp', 'row'), None, ('col', 'chan')), parts along dimension 0
The draws below stay inside these ranges and needn't reach their ends.
There are 2 independent parts, one for each index of `grp`. The reference program is written for one: setup_inputs(seed, part) draws one part's arguments, and reference() takes and returns one part's arrays. A program takes and returns all parts, laid end to end along the dimension named above; an argument that names none is the same for every part. Nothing has to cross between parts.
All inputs are finite; a program needn't handle non-finite values.
Results may differ from the reference program's by a relative error of at most 0.025.
Values may be sent and summed in bfloat16 or wider, within the bound.
No kernel may reach another device: no remote copies, remote signals or barrier semaphores. Data moves between devices by JAX's collectives and lax.ppermute only.
A program may use at most 128 MiB of HBM per device.

```python
import jax
import jax.numpy as jnp
from jax import lax

D = 1024
W = 12
PHYS = 4
S = 16


def with_spikes(values, rng, source, target, shards_of, factor):
    owner, partner = [(jnp.arange(values.shape[dim]) // (values.shape[dim] // shards_of)).reshape([-1 if axis == dim else 1 for axis in range(values.ndim)]) for dim in (source, target)]
    chosen = jax.random.permutation(rng, shards_of)[partner]
    strong = (owner == chosen) | (owner == (partner + shards_of // 2) % shards_of)
    return jnp.where(strong, factor * values, values)


def block_scale(key, extent, shards, least, top_value):
    gain, own = 1.0, jax.random.fold_in(key, 6)
    for dim, parts in shards:
        draws = jnp.exp(jax.random.uniform(jax.random.fold_in(own, dim), (parts,), jnp.float32, least / len(shards), top_value / len(shards)))
        gain = gain * jnp.repeat(draws, extent[dim] // parts).reshape([-1 if axis == dim else 1 for axis in range(len(extent))])
    return gain


def normal_values(stream_key, shape, scale, most, cuts=(), kind=jnp.bfloat16):
    entries = jax.random.normal(stream_key, shape, jnp.float32) * scale
    if len(cuts) > 0:
        entries = block_scale(stream_key, shape, cuts, -0.22, 0.18) * entries
    return jnp.clip(entries, min=-most, max=most).astype(kind)


def gaussian_with(own_key, extent, spread, bound, shards, heavy, held_as=jnp.bfloat16):
    result = spread * jax.random.normal(own_key, extent, jnp.float32)
    if shards:
        result = result * block_scale(own_key, extent, shards, -0.22, 0.18)
    return jnp.clip(with_spikes(result, jax.random.fold_in(own_key, 3), *heavy), -bound, bound).astype(held_as)


def setup_inputs(seed: int = 0, part: int = 0) -> dict:
    arg_keys = jax.random.split(jax.random.key(seed), 6)
    part_keys = jax.random.split(jax.random.fold_in(arg_keys[5], part), 6)
    return {
        "theta": normal_values(part_keys[0], (D, S, D), 1.0, 6.0, ((0, 4), (2, 4))),
        "left_env": gaussian_with(part_keys[1], (D, W, D), D ** -0.5, 0.25, ((0, 4),), (0, 2, 4, 2.0)),
        "right_env": gaussian_with(part_keys[2], (D, W, D), (W * D) ** -0.5, 0.078125, ((2, 4),), (2, 0, 4, 2.0)),
        "mpo_left": normal_values(arg_keys[3], (W, W, PHYS, PHYS), (W * PHYS) ** -0.5, 0.875, (), jnp.float32),
        "mpo_right": normal_values(arg_keys[4], (W, W, PHYS, PHYS), (W * PHYS) ** -0.5, 0.875, (), jnp.float32),
    }


def mpo_product(mpo_left, mpo_right):
    paired = jnp.einsum('wuxs,uvyt->wstxyv', mpo_left, mpo_right, precision=lax.Precision.HIGHEST)
    return paired.reshape(W * PHYS * PHYS, PHYS * PHYS * W).astype(jnp.bfloat16)


def rounded(values):
    return lax.optimization_barrier(values.astype(jnp.bfloat16)).astype(jnp.float32)


def reference(theta, left_env, right_env, mpo_left, mpo_right):
    mpo_pair = mpo_product(mpo_left, mpo_right).astype(jnp.float32)
    theta_wide = theta.astype(jnp.float32)
    right_wide = right_env.astype(jnp.float32)
    stride = min(64, D)
    blocks = D // stride

    def step(total, index):
        begin = (index * stride).astype(jnp.int32)
        left_block = lax.dynamic_slice_in_dim(left_env, begin, stride, 0).astype(jnp.float32)
        section_one = rounded(jnp.einsum('awk,ksb->awsb', left_block, theta_wide))
        section_three = rounded(jnp.einsum('pq,apb->aqb', mpo_pair, section_one.reshape(stride, W * S, D)))
        section_three = section_three.reshape(stride, S, W, D)
        partial_res = jnp.einsum('kvb,asvb->kas', right_wide, section_three).reshape(D, stride * S)
        resid_block = partial_res.astype(jnp.bfloat16)
        back_one = rounded(jnp.einsum('kp,kvb->pvb', rounded(partial_res), right_wide))
        back_one = back_one.reshape(stride, S * W, D)
        back_two = rounded(jnp.einsum('pq,aqb->apb', mpo_pair, back_one)).reshape(stride, W, S, D)
        total = total + jnp.einsum('awk,awsb->ksb', left_block, back_two)
        return total, resid_block

    total, resid_blocks = lax.scan(step, jnp.zeros((D, S, D), jnp.float32), jnp.arange(blocks, dtype=jnp.int32))
    residual = jnp.transpose(resid_blocks, (1, 0, 2)).reshape(D, D * S)
    return residual, total.astype(jnp.bfloat16)
```

```python
import functools

import jax
import jax.numpy as jnp
from jax import lax
from jax.experimental import pallas as pl
from jax.experimental.pallas import tpu as pltpu
from jax.sharding import PartitionSpec as P

BF16 = jnp.bfloat16
F32 = jnp.float32
MIB = 1024 * 1024
LINES = (((1,), (0,)), ((), ()))
ROWS = (((1,), (1,)), ((), ()))
COLS = (((0,), (0,)), ((), ()))
WHOLE = pl.BlockSpec(memory_space=pltpu.VMEM)
ONCE = pl.Buffered(1)


def dot(x, y, dims=LINES):
    return lax.dot_general(x, y, dims, preferred_element_type=F32)


def params(limit=56):
    return pltpu.CompilerParams(vmem_limit_bytes=limit * MIB)


def cost(flops, moved):
    return pl.CostEstimate(flops=int(flops), bytes_accessed=int(moved), transcendentals=0)


def first_kernel(rows_axis, n_rows, channels, width, *refs):
    blocks = refs[: 2 * n_rows - 1]
    left_ref, out_ref, held, sems = refs[2 * n_rows - 1 :]
    depth = blocks[0].shape[0]

    @pl.when(pl.program_id(0) == 0)
    def _():
        row = lax.axis_index(rows_axis)
        for phase in ("start", "wait"):
            for k in range(2 * n_rows - 1):
                source = row + (k - (n_rows - 1))

                @pl.when((source >= 0) & (source < n_rows))
                def _():
                    copy = pltpu.make_async_copy(
                        blocks[k],
                        held.at[pl.ds(pl.multiple_of(source * depth, depth), depth), :],
                        sems.at[k],
                    )
                    getattr(copy, phase)()

    full = dot(left_ref[...], held[...])
    pair = 2 * channels
    count = full.shape[1] // width
    for i in range(full.shape[0] // pair):
        rows = full[i * pair : (i + 1) * pair]
        stacked = jnp.concatenate(
            [rows[:, s * width : (s + 1) * width] for s in range(count)], axis=0
        )
        out_ref[i] = stacked.astype(BF16)


def first(blocks, left, n_rows, channels, width, tile):
    depth, columns = blocks[0].shape
    steps = left.shape[0] // (tile * channels)
    pair_rows = 2 * channels * (columns // width)
    return pl.pallas_call(
        functools.partial(first_kernel, "row", n_rows, channels, width),
        grid=(steps,),
        in_specs=[pl.BlockSpec(memory_space=pl.ANY)] * len(blocks)
        + [pl.BlockSpec((tile * channels, left.shape[1]), lambda i: (i, 0))],
        out_specs=pl.BlockSpec((tile // 2, pair_rows, width), lambda i: (i, 0, 0)),
        out_shape=jax.ShapeDtypeStruct((steps * tile // 2, pair_rows, width), BF16),
        scratch_shapes=[
            pltpu.VMEM((depth * n_rows, columns), BF16),
            pltpu.SemaphoreType.DMA((len(blocks),)),
        ],
        compiler_params=params(),
        cost_estimate=cost(
            2 * left.shape[0] * left.shape[1] * columns,
            2 * (left.size + depth * n_rows * columns + left.shape[0] * columns),
        ),
    )(*blocks, left)


def middle_kernel(n_chunks, channels, phys_pair, *refs):
    chunks = refs[:n_chunks]
    mpo_ref, right_ref = refs[n_chunks : n_chunks + 2]
    outs = refs[n_chunks + 2 : -1]
    third = refs[-1]
    width = chunks[0].shape[2]
    step = 2 * phys_pair
    for i in range(chunks[0].shape[0]):
        stacked = jnp.concatenate([c[i] for c in chunks], axis=0)
        mixed = dot(mpo_ref[...], stacked).astype(BF16)
        for v in range(channels):
            third[i * step : (i + 1) * step, v * width : (v + 1) * width] = mixed[
                v * step : (v + 1) * step
            ]
    height = outs[0].shape[0]
    for k, out in enumerate(outs):
        out[...] = dot(right_ref[k * height : (k + 1) * height], third[...], ROWS).astype(BF16)


def middle(chunks, mpo, right, group, groups, parts, channels, phys_pair, tile):
    pairs, pair_rows, width = chunks[0].shape
    per = pairs // groups
    steps = per // (tile // 2)
    height = right.shape[0] // parts
    columns = per * 2 * phys_pair
    return pl.pallas_call(
        functools.partial(middle_kernel, len(chunks), channels, phys_pair),
        grid=(steps,),
        in_specs=[
            pl.BlockSpec((tile // 2, pair_rows, width), lambda i: (group * steps + i, 0, 0))
        ]
        * len(chunks)
        + [
            pl.BlockSpec(mpo.shape, lambda i: (0, 0), pipeline_mode=ONCE),
            pl.BlockSpec(right.shape, lambda i: (0, 0), pipeline_mode=ONCE),
        ],
        out_specs=[pl.BlockSpec((height, tile * phys_pair), lambda i: (0, i))] * parts,
        out_shape=[jax.ShapeDtypeStruct((height, columns), BF16)] * parts,
        scratch_shapes=[pltpu.VMEM((tile * phys_pair, channels * width), BF16)],
        compiler_params=params(),
        cost_estimate=cost(
            2 * right.size * columns + 2 * per * mpo.size * width,
            2 * (right.size + right.shape[0] * columns + len(chunks) * per * pair_rows * width),
        ),
    )(*chunks, mpo, right)


def back_kernel(channels, phys_pair, *refs):
    parts = refs[:-4]
    mpo_ref, right_ref, out_ref, back = refs[-4:]
    width = right_ref.shape[1] // channels
    step = 2 * phys_pair
    pair = 2 * channels
    joined = jnp.concatenate([p[...] for p in parts], axis=0)
    back[...] = dot(joined, right_ref[...], COLS).astype(BF16)
    for i in range(0, out_ref.shape[0] // pair, 2):
        mixed = []
        for j in (i, i + 1):
            rows = back[j * step : (j + 1) * step, :]
            stacked = jnp.concatenate(
                [rows[:, v * width : (v + 1) * width] for v in range(channels)], axis=0
            )
            mixed.append(dot(mpo_ref[...], stacked))
        for s in range(phys_pair):
            both = jnp.concatenate([m[s * pair : (s + 1) * pair] for m in mixed], axis=0)
            out_ref[i * pair : (i + 2) * pair, s * width : (s + 1) * width] = both.astype(BF16)


def backward(parts, mpo, right, channels, phys_pair, tile):
    columns = parts[0].shape[1]
    bonds = columns // phys_pair
    width = right.shape[1] // channels
    return pl.pallas_call(
        functools.partial(back_kernel, channels, phys_pair),
        grid=(bonds // tile,),
        in_specs=[pl.BlockSpec((p.shape[0], tile * phys_pair), lambda i: (0, i)) for p in parts]
        + [
            pl.BlockSpec(mpo.shape, lambda i: (0, 0), pipeline_mode=ONCE),
            pl.BlockSpec(right.shape, lambda i: (0, 0), pipeline_mode=ONCE),
        ],
        out_specs=pl.BlockSpec((tile * channels, phys_pair * width), lambda i: (i, 0)),
        out_shape=jax.ShapeDtypeStruct((bonds * channels, phys_pair * width), BF16),
        scratch_shapes=[pltpu.VMEM((tile * phys_pair, right.shape[1]), BF16)],
        compiler_params=params(),
        cost_estimate=cost(
            2 * right.size * columns + bonds * mpo.size * width,
            2 * (right.size + right.shape[0] * columns + bonds * channels * phys_pair * width),
        ),
    )(*parts, mpo, right)


def last_kernel(rows_axis, n_rows, n_groups, *refs):
    left_ref = refs[0]
    backs = refs[1 : 1 + n_groups]
    outs = refs[1 + n_groups :]
    row = lax.axis_index(rows_axis)
    height = outs[0].shape[0]
    depth = backs[0].shape[0]
    for d, out in enumerate(outs):
        j = lax.rem(row + d, n_rows)
        rows = pl.ds(pl.multiple_of(j * height, height), height)
        total = None
        for g, back in enumerate(backs):
            term = dot(left_ref[rows, g * depth : (g + 1) * depth], back[...])
            total = term if total is None else total + term
        out[...] = total.astype(BF16)


def last(left_t, backs, chunk, n_chunks, n_rows):
    columns = backs[0].shape[1] // n_chunks
    height = left_t.shape[0] // n_rows
    return pl.pallas_call(
        functools.partial(last_kernel, "row", n_rows, len(backs)),
        grid=(1,),
        in_specs=[pl.BlockSpec(left_t.shape, lambda i: (0, 0), pipeline_mode=ONCE)]
        + [
            pl.BlockSpec((b.shape[0], columns), lambda i: (0, chunk), pipeline_mode=ONCE)
            for b in backs
        ],
        out_specs=[pl.BlockSpec((height, columns), lambda i: (0, 0))] * n_rows,
        out_shape=[jax.ShapeDtypeStruct((height, columns), BF16)] * n_rows,
        compiler_params=params(),
        cost_estimate=cost(
            2 * left_t.size * columns,
            2 * (left_t.size + left_t.shape[1] * columns + left_t.shape[0] * columns),
        ),
    )(left_t, *backs)


def gather_rows(block, n_rows):
    above, below = [], []
    up = down = block
    for t in range(1, n_rows):
        up = lax.ppermute(up, "row", [(r, r + 1) for r in range(t - 1, n_rows - 1)])
        down = lax.ppermute(down, "row", [(r, r - 1) for r in range(1, n_rows - t + 1)])
        above.append(up)
        below.append(down)
    return above[::-1] + [block] + below


def scatter_rows(terms, n_rows):
    up = down = None
    for t in range(1, n_rows):
        mine, other = terms[n_rows - t], terms[t]
        if up is not None:
            mine = (mine.astype(F32) + up.astype(F32)).astype(BF16)
            other = (other.astype(F32) + down.astype(F32)).astype(BF16)
        up = lax.ppermute(mine, "row", [(r, r + 1) for r in range(t)])
        down = lax.ppermute(other, "row", [(n_rows - 1 - r, n_rows - 2 - r) for r in range(t)])
    return terms[0].astype(F32) + up.astype(F32) + down.astype(F32)


def add(x, y):
    return (x.astype(F32) + y.astype(F32)).astype(BF16)


def shards(theta, left_env, right_env, mpo_left, mpo_right):
    bonds, channels, depth = left_env.shape
    phys = mpo_left.shape[2]
    rows, phys_pair, width = theta.shape
    far = right_env.shape[0]
    n_rows = lax.axis_size("row")
    n_col, n_chan = lax.axis_size("col"), lax.axis_size("chan")
    n_blocks = n_col * n_chan
    paired_up = n_col == 2 and n_chan == 2
    tile = min(32, bonds)
    n_chunks = 4
    groups = max(1, min(4, bonds // tile))
    per = phys_pair // n_chunks
    swap = [(0, 1), (1, 0)]

    pieces = [
        theta[:, c * per : (c + 1) * per, :].reshape(rows, per * width) for c in range(n_chunks)
    ]
    gathered = [gather_rows(p, n_rows) for p in pieces]

    paired = jnp.einsum("wuxs,uvyt->wstxyv", mpo_left, mpo_right, precision=lax.Precision.HIGHEST)
    mpo = paired.reshape(channels, phys_pair, phys_pair, channels).astype(BF16)
    twice = jnp.einsum("wsxv,jk->sjwvkx", mpo, jnp.eye(2, dtype=BF16))
    size = 2 * channels * phys_pair
    mpo_back = twice.reshape(size, size)
    mpo_fore = mpo_back.T

    left = left_env.reshape(bonds * channels, depth)
    left_t = left.T
    right = right_env.reshape(far, channels * width)
    if paired_up:
        col, chan = lax.axis_index("col"), lax.axis_index("chan")
        block = right.reshape(2, 2, far // 4, channels * width)
        block = jnp.where(col == 0, block, block[::-1])
        block = jnp.where(chan == 0, block, block[:, ::-1])
        right = block.reshape(far, channels * width)

    ones = [first(g, left, n_rows, channels, width, tile) for g in gathered]

    own, backs = [], []
    for g in range(groups):
        terms = middle(
            ones, mpo_fore, right, g, groups, 2 if paired_up else 1, channels, phys_pair, tile
        )
        if paired_up:
            near = add(terms[0], lax.ppermute(terms[1], "col", swap))
            half = far // 4
            mine = add(near[:half], lax.ppermute(near[half:], "chan", swap))
            across = lax.ppermute(mine, "chan", swap)
            parts = [mine, across, lax.ppermute(mine, "col", swap), lax.ppermute(across, "col", swap)]
        else:
            mine = lax.psum_scatter(terms[0], ("col", "chan"), scatter_dimension=0, tiled=True)
            parts = [lax.all_gather(mine, ("col", "chan"), axis=0, tiled=True)]
        own.append(mine)
        backs.append(backward(parts, mpo_back, right, channels, phys_pair, tile))

    products = []
    for c in range(n_chunks):
        total = scatter_rows(last(left_t, backs, c, n_chunks, n_rows), n_rows)
        products.append(total.astype(BF16).reshape(rows, per, width))
    return jnp.concatenate(own, axis=1), jnp.concatenate(products, axis=1)


def solution(mesh):
    in_specs = (
        P(("grp", "row"), None, ("col", "chan")),
        P(("grp", "row"), None, None),
        P("grp", None, ("col", "chan")),
        P(),
        P(),
    )
    out_specs = (P(("grp", "col", "chan"), "row"), P(("grp", "row"), None, ("col", "chan")))
    return jax.shard_map(shards, mesh=mesh, in_specs=in_specs, out_specs=out_specs, check_vma=False)
```

```python
import functools

import jax
import jax.numpy as jnp
from jax import lax
from jax.experimental import pallas as pl
from jax.experimental.pallas import tpu as pltpu
from jax.sharding import PartitionSpec as P

BF16 = jnp.bfloat16
F32 = jnp.float32
MIB = 1024 * 1024
LINES = (((1,), (0,)), ((), ()))
ROWS = (((1,), (1,)), ((), ()))
COLS = (((0,), (0,)), ((), ()))
ANY = pl.BlockSpec(memory_space=pl.ANY)
ONCE = pl.Buffered(1)


def dot(x, y, dims=LINES):
    return lax.dot_general(x, y, dims, preferred_element_type=F32)


def params(limit=56):
    return pltpu.CompilerParams(vmem_limit_bytes=limit * MIB)


def cost(flops, moved):
    return pl.CostEstimate(flops=int(flops), bytes_accessed=int(moved), transcendentals=0)


def run(copies):
    for condition, copy in copies:
        pl.when(condition)(copy.start)
    for condition, copy in copies:
        pl.when(condition)(copy.wait)


def theta_copies(blocks, held, sems, n_rows):
    depth = blocks[0].shape[0]
    row = lax.axis_index("row")
    copies = []
    for k, block in enumerate(blocks):
        source = row + (k - (n_rows - 1))
        target = held.at[pl.ds(pl.multiple_of(source * depth, depth), depth), :]
        copies.append(
            ((source >= 0) & (source < n_rows), pltpu.make_async_copy(block, target, sems.at[k]))
        )
    return copies


def right_copies(right, held, sems, half, lanes):
    return [
        (
            True,
            pltpu.make_async_copy(
                right.at[v, :, pl.ds(half * lanes, lanes)],
                held.at[:, pl.ds(v * lanes, lanes)],
                sems.at[v],
            ),
        )
        for v in range(right.shape[0])
    ]


def block_of(k):
    n_col, n_chan = lax.axis_size("col"), lax.axis_size("chan")
    col = lax.rem(lax.axis_index("col") + k // n_chan, n_col)
    return col * n_chan + lax.rem(lax.axis_index("chan") + k % n_chan, n_chan)


def order_kernel(env_ref, order_ref, left_ref, turned_ref):
    env = env_ref[...].reshape(order_ref.shape[0], env_ref.shape[2])
    left_ref[...] = dot(order_ref[...], env).astype(BF16)
    turned_ref[...] = dot(env, order_ref[...], (((0,), (1,)), ((), ()))).astype(BF16)


def ordered(env, tile):
    channels, bonds, depth = env.shape
    size = tile * channels
    index = jnp.arange(size)
    wanted = (index % channels) * tile + index // channels
    order = (wanted[:, None] == index[None, :]).astype(BF16)
    return pl.pallas_call(
        order_kernel,
        grid=(bonds // tile,),
        in_specs=[
            pl.BlockSpec((channels, tile, depth), lambda i: (0, i, 0)),
            pl.BlockSpec((size, size), lambda i: (0, 0)),
        ],
        out_specs=[
            pl.BlockSpec((size, depth), lambda i: (i, 0)),
            pl.BlockSpec((depth, size), lambda i: (0, i)),
        ],
        out_shape=[
            jax.ShapeDtypeStruct((bonds * channels, depth), BF16),
            jax.ShapeDtypeStruct((depth, bonds * channels), BF16),
        ],
        compiler_params=params(),
        cost_estimate=cost(4 * size * env.size, 6 * env.size),
    )(env, order)


def fore_kernel(n_rows, half, has_total, n_outs, n_deps, *refs):
    refs = list(refs)
    blocks = refs[: 2 * n_rows - 1]
    left_ref, mpo_ref, right = refs[2 * n_rows - 1 : 2 * n_rows + 2]
    rest = refs[2 * n_rows + 2 :]
    total_ref = rest.pop(0) if has_total else None
    del rest[:n_deps]
    outs = rest[:n_outs]
    held, right_held, ones, threes, acc, block_sems, right_sems = rest[n_outs:]
    channels = right.shape[0]
    lanes = right_held.shape[1] // channels
    phys_pair = held.shape[1] // lanes
    pair, step = 2 * channels, 2 * phys_pair
    pairs = left_ref.shape[0] // pair

    @pl.when(pl.program_id(0) == 0)
    def _():
        run(
            theta_copies(blocks, held, block_sems, n_rows)
            + right_copies(right, right_held, right_sems, half, lanes)
        )

    full = dot(left_ref[...], held[...])
    for i in range(pairs):
        for s in range(0, phys_pair, 2):
            both = [
                full[i * pair : (i + 1) * pair, q * lanes : (q + 1) * lanes] for q in (s, s + 1)
            ]
            ones[s * pair : (s + 2) * pair, i * lanes : (i + 1) * lanes] = jnp.concatenate(
                both, axis=0
            ).astype(BF16)
    mixed = dot(mpo_ref[...], ones[...]).astype(BF16)
    for i in range(pairs):
        for v in range(channels):
            threes[i * step : (i + 1) * step, v * lanes : (v + 1) * lanes] = mixed[
                v * step : (v + 1) * step, i * lanes : (i + 1) * lanes
            ]
    part = dot(right_held[...], threes[...], ROWS)
    if has_total:
        part = part + total_ref[...]
    if n_outs == 1:
        outs[0][...] = part.astype(outs[0].dtype)
    else:
        acc[...] = part
        n_blocks = lax.axis_size("col") * lax.axis_size("chan")
        height = acc.shape[0] // n_blocks
        per = n_blocks // n_outs
        for k in range(n_blocks):
            rows = pl.ds(pl.multiple_of(block_of(k) * height, height), height)
            first = k % per * height
            outs[k // per][first : first + height] = acc[rows].astype(BF16)


def fore(blocks, left, mpo, right, total, half, lanes, group, groups, n_outs, kind, tile, deps):
    depth, columns = blocks[0].shape
    n_rows = (len(blocks) + 1) // 2
    channels, far, _ = right.shape
    phys_pair = columns // lanes
    bonds = left.shape[0] // channels // groups
    steps = bonds // tile
    has_total = total is not None
    acc_spec = pl.BlockSpec((far, tile * phys_pair), lambda i: (0, group * steps + i))
    return pl.pallas_call(
        functools.partial(fore_kernel, n_rows, half, has_total, n_outs, len(deps)),
        grid=(steps,),
        in_specs=[ANY] * len(blocks)
        + [
            pl.BlockSpec((tile * channels, left.shape[1]), lambda i: (group * steps + i, 0)),
            pl.BlockSpec(mpo.shape, lambda i: (0, 0)),
            ANY,
        ]
        + [acc_spec] * has_total
        + [ANY] * len(deps),
        out_specs=[pl.BlockSpec((far // n_outs, tile * phys_pair), lambda i: (0, i))] * n_outs,
        out_shape=[jax.ShapeDtypeStruct((far // n_outs, bonds * phys_pair), kind)] * n_outs,
        scratch_shapes=[
            pltpu.VMEM((depth * n_rows, columns), BF16),
            pltpu.VMEM((far, channels * lanes), BF16),
            pltpu.VMEM((2 * channels * phys_pair, tile // 2 * lanes), BF16),
            pltpu.VMEM((tile * phys_pair, channels * lanes), BF16),
            pltpu.VMEM((far, tile * phys_pair) if n_outs > 1 else (8, 128), F32),
            pltpu.SemaphoreType.DMA((len(blocks),)),
            pltpu.SemaphoreType.DMA((channels,)),
        ],
        compiler_params=params(),
        cost_estimate=cost(
            2 * bonds * phys_pair * lanes * channels * (left.shape[1] + far)
            + bonds * mpo.size * lanes,
            2 * (depth * n_rows * columns + far * channels * lanes + bonds * channels * depth)
            + 4 * far * bonds * phys_pair,
        ),
    )(*blocks, left, mpo, right, *([total] if has_total else []), *deps)


def back_kernel(n_parts, half, scattered, n_deps, *refs):
    parts = refs[:n_parts]
    mpo_ref, right = refs[n_parts : n_parts + 2]
    out_ref, right_held, joined, ones, right_sems = refs[n_parts + 2 + n_deps :]
    channels = right.shape[0]
    lanes = right_held.shape[1] // channels
    phys_pair = out_ref.shape[1] // lanes
    pair, step = 2 * channels, 2 * phys_pair
    pairs = out_ref.shape[0] // pair

    @pl.when(pl.program_id(0) == 0)
    def _():
        run(right_copies(right, right_held, right_sems, half, lanes))

    height = parts[0].shape[0]
    for k, part in enumerate(parts):
        place = block_of(k) if scattered else k
        joined[pl.ds(pl.multiple_of(place * height, height), height), :] = part[...]
    full = dot(joined[...], right_held[...], COLS).astype(BF16)
    for i in range(pairs):
        for v in range(channels):
            ones[v * step : (v + 1) * step, i * lanes : (i + 1) * lanes] = full[
                i * step : (i + 1) * step, v * lanes : (v + 1) * lanes
            ]
    mixed = dot(mpo_ref[...], ones[...])
    for i in range(0, pairs, 2):
        for s in range(phys_pair):
            both = [
                mixed[s * pair : (s + 1) * pair, j * lanes : (j + 1) * lanes] for j in (i, i + 1)
            ]
            out_ref[i * pair : (i + 2) * pair, s * lanes : (s + 1) * lanes] = jnp.concatenate(
                both, axis=0
            ).astype(BF16)


def back(parts, mpo, right, half, lanes, phys_pair, scattered, tile, deps):
    columns = parts[0].shape[1]
    bonds = columns // phys_pair
    channels, far, _ = right.shape
    return pl.pallas_call(
        functools.partial(back_kernel, len(parts), half, scattered, len(deps)),
        grid=(bonds // tile,),
        in_specs=[pl.BlockSpec((p.shape[0], tile * phys_pair), lambda i: (0, i)) for p in parts]
        + [pl.BlockSpec(mpo.shape, lambda i: (0, 0)), ANY]
        + [ANY] * len(deps),
        out_specs=pl.BlockSpec((tile * channels, phys_pair * lanes), lambda i: (i, 0)),
        out_shape=jax.ShapeDtypeStruct((bonds * channels, phys_pair * lanes), BF16),
        scratch_shapes=[
            pltpu.VMEM((far, channels * lanes), BF16),
            pltpu.VMEM((far, tile * phys_pair), BF16),
            pltpu.VMEM((2 * channels * phys_pair, tile // 2 * lanes), BF16),
            pltpu.SemaphoreType.DMA((channels,)),
        ],
        compiler_params=params(),
        cost_estimate=cost(
            2 * far * channels * lanes * columns + bonds * mpo.size * lanes,
            2 * (far * channels * lanes + far * columns + bonds * channels * phys_pair * lanes),
        ),
    )(*parts, mpo, right, *deps)


def last_kernel(n_rows, n_groups, n_deps, *refs):
    left_ref = refs[0]
    backs = refs[1 : 1 + n_groups]
    outs = refs[1 + n_groups + n_deps : -1]
    acc = refs[-1]
    height = outs[0].shape[0]
    depth = backs[0].shape[0]
    for g, part in enumerate(backs):
        term = dot(left_ref[:, g * depth : (g + 1) * depth], part[...])
        if g == 0:
            acc[...] = term
        else:
            acc[...] += term
    for d, out in enumerate(outs):
        j = lax.rem(lax.axis_index("row") + d, n_rows)
        out[...] = acc[pl.ds(pl.multiple_of(j * height, height), height), :].astype(BF16)


def last(left_t, backs, chunk, n_chunks, n_rows, deps):
    columns = backs[0].shape[1] // n_chunks
    steps = 2
    height = left_t.shape[0] // n_rows
    return pl.pallas_call(
        functools.partial(last_kernel, n_rows, len(backs), len(deps)),
        grid=(steps,),
        in_specs=[pl.BlockSpec(left_t.shape, lambda i: (0, 0), pipeline_mode=ONCE)]
        + [
            pl.BlockSpec((b.shape[0], columns // steps), lambda i: (0, chunk * steps + i))
            for b in backs
        ]
        + [ANY] * len(deps),
        out_specs=[pl.BlockSpec((height, columns // steps), lambda i: (0, i))] * n_rows,
        out_shape=[jax.ShapeDtypeStruct((height, columns), BF16)] * n_rows,
        scratch_shapes=[pltpu.VMEM((left_t.shape[0], columns // steps), F32)],
        compiler_params=params(),
        cost_estimate=cost(
            2 * left_t.size * columns,
            2 * (left_t.size + left_t.shape[1] * columns + left_t.shape[0] * columns),
        ),
    )(left_t, *backs, *deps)


def gather_rows(block, n_rows):
    above, below = [], []
    up = down = block
    for t in range(1, n_rows):
        up = lax.ppermute(up, "row", [(r, r + 1) for r in range(t - 1, n_rows - 1)])
        down = lax.ppermute(down, "row", [(r, r - 1) for r in range(1, n_rows - t + 1)])
        above.append(up)
        below.append(down)
    return above[::-1] + [block] + below


def scatter_rows(terms, n_rows):
    up = down = None
    for t in range(1, n_rows):
        mine, other = terms[n_rows - t], terms[t]
        if up is not None:
            mine = (mine.astype(F32) + up.astype(F32)).astype(BF16)
            other = (other.astype(F32) + down.astype(F32)).astype(BF16)
        up = lax.ppermute(mine, "row", [(r, r + 1) for r in range(t)])
        down = lax.ppermute(other, "row", [(n_rows - 1 - r, n_rows - 2 - r) for r in range(t)])
        if t == 1:
            early = up
    return terms[0].astype(F32) + up.astype(F32) + down.astype(F32), early


def add(x, y):
    return (x.astype(F32) + y.astype(F32)).astype(BF16)


def shards(theta, left_env, right_env, mpo_left, mpo_right):
    bonds, channels, depth = left_env.shape
    rows, phys_pair, width = theta.shape
    n_rows = lax.axis_size("row")
    scattered = lax.axis_size("col") == 2 and lax.axis_size("chan") == 2
    tile = min(32, bonds)
    lanes = min(128, width)
    halves = width // lanes
    groups = max(1, min(4, bonds // tile))
    swap = [(0, 1), (1, 0)]

    pieces = [
        theta[:, :, h * lanes : (h + 1) * lanes].reshape(rows, phys_pair * lanes)
        for h in range(halves)
    ]
    gathered = [gather_rows(p, n_rows) for p in pieces]

    paired = jnp.einsum("wuxs,uvyt->wstxyv", mpo_left, mpo_right, precision=lax.Precision.HIGHEST)
    mpo = paired.reshape(channels, phys_pair, phys_pair, channels).astype(BF16)
    twice = jnp.einsum("wsxv,jk->sjwvkx", mpo, jnp.eye(2, dtype=BF16))
    size = 2 * channels * phys_pair
    mpo_back = twice.reshape(size, size)
    mpo_fore = mpo_back.T

    left, left_t = ordered(left_env.transpose(1, 0, 2), tile)
    right = right_env.transpose(1, 0, 2)

    total = None
    for h in range(halves - 1):
        (total,) = fore(
            gathered[h], left, mpo_fore, right, total, h, lanes, 0, 1, 1, F32, tile, []
        )

    own, everyone = [], []
    for g in range(groups):
        terms = fore(
            gathered[-1], left, mpo_fore, right, total, halves - 1, lanes, g, groups,
            2 if scattered else 1, BF16, tile, [own[g - 2]] if g > 1 else [],
        )
        if scattered:
            near = add(terms[0], lax.ppermute(terms[1], "col", swap))
            half = near.shape[0] // 2
            mine = add(near[:half], lax.ppermute(near[half:], "chan", swap))
            across = lax.ppermute(mine, "chan", swap)
            parts = [mine, across] + [lax.ppermute(p, "col", swap) for p in (mine, across)]
        else:
            mine = lax.psum_scatter(terms[0], ("col", "chan"), scatter_dimension=0, tiled=True)
            parts = [lax.all_gather(mine, ("col", "chan"), axis=0, tiled=True)]
        own.append(mine)
        everyone.append(parts)

    n_chunks = 2
    per = phys_pair // n_chunks
    products, deps, early = [], [], []
    for h in range(halves):
        backs = [
            back(parts, mpo_back, right, h, lanes, phys_pair, scattered, tile, deps)
            for parts in everyone
        ]
        chunks = []
        for c in range(n_chunks):
            terms = last(left_t, backs, c, n_chunks, n_rows, early[-2:-1])
            deps = [terms[0]]
            chunk, first = scatter_rows(terms, n_rows)
            early.append(first)
            chunks.append(chunk.astype(BF16).reshape(rows, per, lanes))
        products.append(jnp.concatenate(chunks, axis=1))
    return jnp.concatenate(own, axis=1), jnp.concatenate(products, axis=2)


def solution(mesh):
    in_specs = (
        P(("grp", "row"), None, ("col", "chan")),
        P(("grp", "row"), None, None),
        P("grp", None, ("col", "chan")),
        P(),
        P(),
    )
    out_specs = (P(("grp", "col", "chan"), "row"), P(("grp", "row"), None, ("col", "chan")))
    return jax.shard_map(shards, mesh=mesh, in_specs=in_specs, out_specs=out_specs, check_vma=False)
```

```python
import functools

import jax
import jax.numpy as jnp
from jax import lax
from jax.experimental import pallas as pl
from jax.experimental.pallas import tpu as pltpu
from jax.sharding import PartitionSpec as P

BF16 = jnp.bfloat16
F32 = jnp.float32
MIB = 1024 * 1024
LINES = (((1,), (0,)), ((), ()))
ROWS = (((1,), (1,)), ((), ()))
COLS = (((0,), (0,)), ((), ()))
ANY = pl.BlockSpec(memory_space=pl.ANY)
ONCE = pl.Buffered(1)


def dot(x, y, dims=LINES):
    return lax.dot_general(x, y, dims, preferred_element_type=F32)


def params(limit=56):
    return pltpu.CompilerParams(vmem_limit_bytes=limit * MIB)


def cost(flops, moved):
    return pl.CostEstimate(flops=int(flops) // 16, bytes_accessed=int(moved) // 16, transcendentals=0)


def run(copies):
    for condition, copy in copies:
        pl.when(condition)(copy.start)
    for condition, copy in copies:
        pl.when(condition)(copy.wait)


def theta_copies(blocks, held, sems, n_rows):
    depth = blocks[0].shape[0]
    row = lax.axis_index("row")
    copies = []
    for k, block in enumerate(blocks):
        source = row + (k - (n_rows - 1))
        target = held.at[pl.ds(pl.multiple_of(source * depth, depth), depth), :]
        copies.append(
            ((source >= 0) & (source < n_rows), pltpu.make_async_copy(block, target, sems.at[k]))
        )
    return copies


def right_copies(right, held, sems, half, lanes):
    return [
        (
            True,
            pltpu.make_async_copy(
                right.at[v, :, pl.ds(half * lanes, lanes)],
                held.at[:, pl.ds(v * lanes, lanes)],
                sems.at[v],
            ),
        )
        for v in range(right.shape[0])
    ]


def block_of(k):
    n_col, n_chan = lax.axis_size("col"), lax.axis_size("chan")
    col = lax.rem(lax.axis_index("col") + k // n_chan, n_col)
    return col * n_chan + lax.rem(lax.axis_index("chan") + k % n_chan, n_chan)


def order_kernel(env_ref, order_ref, left_ref, turned_ref):
    env = env_ref[...].reshape(order_ref.shape[0], env_ref.shape[2])
    left_ref[...] = dot(order_ref[...], env).astype(BF16)
    turned_ref[...] = dot(env, order_ref[...], (((0,), (1,)), ((), ()))).astype(BF16)


def ordered(env, tile):
    channels, bonds, depth = env.shape
    size = tile * channels
    index = jnp.arange(size)
    wanted = (index % channels) * tile + index // channels
    order = (wanted[:, None] == index[None, :]).astype(BF16)
    return pl.pallas_call(
        order_kernel,
        grid=(bonds // tile,),
        in_specs=[
            pl.BlockSpec((channels, tile, depth), lambda i: (0, i, 0)),
            pl.BlockSpec((size, size), lambda i: (0, 0)),
        ],
        out_specs=[
            pl.BlockSpec((size, depth), lambda i: (i, 0)),
            pl.BlockSpec((depth, size), lambda i: (0, i)),
        ],
        out_shape=[
            jax.ShapeDtypeStruct((bonds * channels, depth), BF16),
            jax.ShapeDtypeStruct((depth, bonds * channels), BF16),
        ],
        compiler_params=params(),
        cost_estimate=cost(4 * size * env.size, 6 * env.size),
    )(env, order)


def fore_kernel(n_rows, half, has_total, n_outs, *refs):
    refs = list(refs)
    blocks = refs[: 2 * n_rows - 1]
    left_ref, mpo_ref, right = refs[2 * n_rows - 1 : 2 * n_rows + 2]
    rest = refs[2 * n_rows + 2 :]
    total_ref = rest.pop(0) if has_total else None
    outs = rest[:n_outs]
    held, right_held, ones, threes, acc, block_sems, right_sems = rest[n_outs:]
    channels = right.shape[0]
    lanes = right_held.shape[1] // channels
    phys_pair = held.shape[1] // lanes
    pair, step = 2 * channels, 2 * phys_pair
    pairs = left_ref.shape[0] // pair

    @pl.when(pl.program_id(0) == 0)
    def _():
        run(
            theta_copies(blocks, held, block_sems, n_rows)
            + right_copies(right, right_held, right_sems, half, lanes)
        )

    full = dot(left_ref[...], held[...])
    for i in range(pairs):
        for s in range(0, phys_pair, 2):
            both = [
                full[i * pair : (i + 1) * pair, q * lanes : (q + 1) * lanes] for q in (s, s + 1)
            ]
            ones[s * pair : (s + 2) * pair, i * lanes : (i + 1) * lanes] = jnp.concatenate(
                both, axis=0
            ).astype(BF16)
    mixed = dot(mpo_ref[...], ones[...]).astype(BF16)
    for i in range(pairs):
        for v in range(channels):
            threes[i * step : (i + 1) * step, v * lanes : (v + 1) * lanes] = mixed[
                v * step : (v + 1) * step, i * lanes : (i + 1) * lanes
            ]
    part = dot(right_held[...], threes[...], ROWS)
    if has_total:
        part = part + total_ref[...]
    if n_outs == 1:
        outs[0][...] = part.astype(outs[0].dtype)
    else:
        acc[...] = part
        n_blocks = lax.axis_size("col") * lax.axis_size("chan")
        height = acc.shape[0] // n_blocks
        per = n_blocks // n_outs
        for k in range(n_blocks):
            rows = pl.ds(pl.multiple_of(block_of(k) * height, height), height)
            first = k % per * height
            outs[k // per][first : first + height] = acc[rows].astype(BF16)


def fore(
    blocks, left, mpo, right, total, place, half, lanes, group, groups, n_outs, kind, tile
):
    depth, columns = blocks[0].shape
    n_rows = (len(blocks) + 1) // 2
    channels, far, _ = right.shape
    phys_pair = columns // lanes
    bonds = left.shape[0] // channels // groups
    steps = bonds // tile
    has_total = total is not None
    acc_spec = pl.BlockSpec((far, tile * phys_pair), lambda i: (0, place * steps + i))
    return pl.pallas_call(
        functools.partial(fore_kernel, n_rows, half, has_total, n_outs),
        grid=(steps,),
        in_specs=[ANY] * len(blocks)
        + [
            pl.BlockSpec((tile * channels, left.shape[1]), lambda i: (group * steps + i, 0)),
            pl.BlockSpec(mpo.shape, lambda i: (0, 0)),
            ANY,
        ]
        + [acc_spec] * has_total,
        out_specs=[pl.BlockSpec((far // n_outs, tile * phys_pair), lambda i: (0, i))] * n_outs,
        out_shape=[jax.ShapeDtypeStruct((far // n_outs, bonds * phys_pair), kind)] * n_outs,
        scratch_shapes=[
            pltpu.VMEM((depth * n_rows, columns), BF16),
            pltpu.VMEM((far, channels * lanes), BF16),
            pltpu.VMEM((2 * channels * phys_pair, tile // 2 * lanes), BF16),
            pltpu.VMEM((tile * phys_pair, channels * lanes), BF16),
            pltpu.VMEM((far, tile * phys_pair) if n_outs > 1 else (8, 128), F32),
            pltpu.SemaphoreType.DMA((len(blocks),)),
            pltpu.SemaphoreType.DMA((channels,)),
        ],
        compiler_params=params(),
        cost_estimate=cost(
            2 * bonds * phys_pair * lanes * channels * (left.shape[1] + far)
            + bonds * mpo.size * lanes,
            2 * (depth * n_rows * columns + far * channels * lanes + bonds * channels * depth)
            + 4 * far * bonds * phys_pair,
        ),
    )(*blocks, left, mpo, right, *([total] if has_total else []))


def back_kernel(n_parts, half, scattered, *refs):
    parts = refs[:n_parts]
    mpo_ref, right = refs[n_parts : n_parts + 2]
    out_ref, right_held, joined, ones, right_sems = refs[-5:]
    channels = right.shape[0]
    lanes = right_held.shape[1] // channels
    phys_pair = out_ref.shape[1] // lanes
    pair, step = 2 * channels, 2 * phys_pair
    pairs = out_ref.shape[0] // pair

    @pl.when(pl.program_id(0) == 0)
    def _():
        run(right_copies(right, right_held, right_sems, half, lanes))

    height = parts[0].shape[0]
    for k, part in enumerate(parts):
        place = block_of(k) if scattered else k
        joined[pl.ds(pl.multiple_of(place * height, height), height), :] = part[...]
    full = dot(joined[...], right_held[...], COLS).astype(BF16)
    for i in range(pairs):
        for v in range(channels):
            ones[v * step : (v + 1) * step, i * lanes : (i + 1) * lanes] = full[
                i * step : (i + 1) * step, v * lanes : (v + 1) * lanes
            ]
    mixed = dot(mpo_ref[...], ones[...])
    for i in range(0, pairs, 2):
        for s in range(phys_pair):
            both = [
                mixed[s * pair : (s + 1) * pair, j * lanes : (j + 1) * lanes] for j in (i, i + 1)
            ]
            out_ref[i * pair : (i + 2) * pair, s * lanes : (s + 1) * lanes] = jnp.concatenate(
                both, axis=0
            ).astype(BF16)


def back(parts, mpo, right, buffer, group, groups, half, lanes, phys_pair, scattered, tile):
    columns = parts[0].shape[1]
    bonds = columns // phys_pair
    channels, far, _ = right.shape
    steps = bonds // tile
    buffers = [] if buffer is None else [buffer]
    return pl.pallas_call(
        functools.partial(back_kernel, len(parts), half, scattered),
        grid=(steps,),
        input_output_aliases={} if buffer is None else {len(parts) + 2: 0},
        in_specs=[pl.BlockSpec((p.shape[0], tile * phys_pair), lambda i: (0, i)) for p in parts]
        + [pl.BlockSpec(mpo.shape, lambda i: (0, 0)), ANY]
        + [ANY] * len(buffers),
        out_specs=pl.BlockSpec(
            (tile * channels, phys_pair * lanes), lambda i: (group * steps + i, 0)
        ),
        out_shape=jax.ShapeDtypeStruct((groups * bonds * channels, phys_pair * lanes), BF16),
        scratch_shapes=[
            pltpu.VMEM((far, channels * lanes), BF16),
            pltpu.VMEM((far, tile * phys_pair), BF16),
            pltpu.VMEM((2 * channels * phys_pair, tile // 2 * lanes), BF16),
            pltpu.SemaphoreType.DMA((channels,)),
        ],
        compiler_params=params(),
        cost_estimate=cost(
            2 * far * channels * lanes * columns + bonds * mpo.size * lanes,
            2 * (far * channels * lanes + far * columns + bonds * channels * phys_pair * lanes),
        ),
    )(*parts, mpo, right, *buffers)


def last_kernel(n_rows, *refs):
    left_ref, back_ref = refs[:2]
    outs = refs[2:-1]
    acc = refs[-1]
    height = outs[0].shape[0]
    acc[...] = dot(left_ref[...], back_ref[...])
    for d, out in enumerate(outs):
        j = lax.rem(lax.axis_index("row") + d, n_rows)
        out[...] = acc[pl.ds(pl.multiple_of(j * height, height), height), :].astype(BF16)


def last(left_t, backs, chunk, n_chunks, n_rows):
    columns = backs.shape[1] // n_chunks
    steps = 2
    height = left_t.shape[0] // n_rows
    return pl.pallas_call(
        functools.partial(last_kernel, n_rows),
        grid=(steps,),
        in_specs=[
            pl.BlockSpec(left_t.shape, lambda i: (0, 0), pipeline_mode=ONCE),
            pl.BlockSpec((backs.shape[0], columns // steps), lambda i: (0, chunk * steps + i)),
        ],
        out_specs=[pl.BlockSpec((height, columns // steps), lambda i: (0, i))] * n_rows,
        out_shape=[jax.ShapeDtypeStruct((height, columns), BF16)] * n_rows,
        scratch_shapes=[pltpu.VMEM((left_t.shape[0], columns // steps), F32)],
        compiler_params=params(),
        cost_estimate=cost(
            2 * left_t.size * columns,
            2 * (left_t.size + left_t.shape[1] * columns + left_t.shape[0] * columns),
        ),
    )(left_t, backs)


def after(arrays, *deps):
    return lax.optimization_barrier((arrays, deps))[0]


def gather_round(up, down, t, n_rows):
    up = lax.ppermute(up, "row", [(r, r + 1) for r in range(t - 1, n_rows - 1)])
    down = lax.ppermute(down, "row", [(r, r - 1) for r in range(1, n_rows - t + 1)])
    return up, down


def scatter_rows(terms, n_rows):
    up = down = None
    seen = []
    for t in range(1, n_rows):
        mine, other = terms[n_rows - t], terms[t]
        if up is not None:
            mine, other = add(mine, up), add(other, down)
        mine, other = lax.optimization_barrier((mine, other))
        up = lax.ppermute(mine, "row", [(r, r + 1) for r in range(t)])
        down = lax.ppermute(other, "row", [(n_rows - 1 - r, n_rows - 2 - r) for r in range(t)])
        seen.append([up, down])
    return terms[0].astype(F32) + up.astype(F32) + down.astype(F32), seen


def add(x, y):
    return (x.astype(F32) + y.astype(F32)).astype(BF16)


def shards(theta, left_env, right_env, mpo_left, mpo_right):
    bonds, channels, depth = left_env.shape
    rows, phys_pair, width = theta.shape
    n_rows = lax.axis_size("row")
    scattered = lax.axis_size("col") == 2 and lax.axis_size("chan") == 2
    tile = min(32, bonds)
    lanes = min(128, width)
    halves = width // lanes
    groups = max(1, min(4, bonds // tile))
    swap = [(0, 1), (1, 0)]

    paired = jnp.einsum("wuxs,uvyt->wstxyv", mpo_left, mpo_right, precision=lax.Precision.HIGHEST)
    mpo = paired.reshape(channels, phys_pair, phys_pair, channels).astype(BF16)
    twice = jnp.einsum("wsxv,jk->sjwvkx", mpo, jnp.eye(2, dtype=BF16))
    size = 2 * channels * phys_pair
    mpo_back = twice.reshape(size, size)
    mpo_fore = mpo_back.T

    left, left_t = ordered(left_env.transpose(1, 0, 2), tile)
    right = right_env.transpose(1, 0, 2)

    totals, cuts = [None], 2 if groups % 2 == 0 else 1
    blocks, before, final = [], (), ()
    for h in range(halves):
        prior, new = blocks, []

        def forward(*deps):
            return fore(
                after(prior, *deps), left, mpo_fore, right, totals[len(new) % len(totals)], 0,
                h - 1, lanes, len(new), cuts, 1, F32, tile,
            )

        up = down = theta[:, :, h * lanes : (h + 1) * lanes].reshape(rows, phys_pair * lanes)
        blocks = [up]
        for t in range(1, n_rows):
            waits = before if t == 1 else final if t == 2 else new[t - 3 : t - 2]
            if h == 0 and t > 1:
                waits = [left, left_t] if t == 2 else [mpo_fore, mpo_back]
            up, down = after((up, down), *waits)
            before = (up, down)
            up, down = gather_round(up, down, t, n_rows)
            blocks = [up] + blocks + [down]
            if h > 0 and len(new) < cuts:
                new += forward(up, down)
        final = (up, down)
        if h > 0:
            while len(new) < cuts:
                new += forward()
            totals = new

    own, everyone, waits = [], [], []
    if halves > 1:
        blocks, totals = lax.optimization_barrier((blocks, totals))
    for g in range(groups):
        if g > 0:
            blocks = after(blocks, *waits)
        terms = fore(
            blocks, left, mpo_fore, right, totals[g * len(totals) // groups],
            g % (groups // len(totals)), halves - 1, lanes, g, groups, 2 if scattered else 1, BF16,
            tile,
        )
        if scattered:
            near = add(terms[0], lax.ppermute(terms[1], "col", swap))
            half = near.shape[0] // 2
            mine = add(near[:half], lax.ppermute(near[half:], "chan", swap))
            across = lax.ppermute(mine, "chan", swap)
            parts = [mine, across] + [lax.ppermute(p, "col", swap) for p in (mine, across)]
        else:
            near = terms[0]
            mine = lax.psum_scatter(near, ("col", "chan"), scatter_dimension=0, tiled=True)
            parts = [lax.all_gather(mine, ("col", "chan"), axis=0, tiled=True)]
        waits = [near] + own[-1:] + [p[-1] for p in everyone[-2:-1]]
        own.append(mine)
        everyone.append(parts)

    n_chunks = 2
    per = phys_pair // n_chunks
    products, seen = [], []
    for h in range(halves):
        backs = None
        for g, parts in enumerate(everyone):
            if h > 0:
                waits = [terms[0]] if g < groups // 2 else seen[-1][0] + seen[-2][0]
                parts = after(parts, *waits)
            elif g == 0:
                parts = after(parts, *waits)
            else:
                parts = after(parts, *own[groups // 2 : groups // 2 + g])
            backs = back(
                parts, mpo_back, right, backs, g, groups, h, lanes, phys_pair, scattered, tile
            )
        if h > 0:
            backs = after(backs, *[x for rounds in seen[-2:] for x in rounds[min(1, n_rows - 2)]])
        for c in range(n_chunks):
            if c > 0:
                backs = after(backs, *terms)
            terms = last(left_t, backs, c, n_chunks, n_rows)
            chunk, rounds = scatter_rows(terms, n_rows)
            seen.append(rounds)
            products.append(chunk.astype(BF16).reshape(rows, per, lanes))
    products = [
        jnp.concatenate(products[h * n_chunks : (h + 1) * n_chunks], axis=1) for h in range(halves)
    ]
    return jnp.concatenate(own, axis=1), jnp.concatenate(products, axis=2)


def solution(mesh):
    in_specs = (
        P(("grp", "row"), None, ("col", "chan")),
        P(("grp", "row"), None, None),
        P("grp", None, ("col", "chan")),
        P(),
        P(),
    )
    out_specs = (P(("grp", "col", "chan"), "row"), P(("grp", "row"), None, ("col", "chan")))
    return jax.shard_map(shards, mesh=mesh, in_specs=in_specs, out_specs=out_specs, check_vma=False)
```

```python
import functools

import jax
import jax.numpy as jnp
from jax import lax
from jax.experimental import pallas as pl
from jax.experimental.pallas import tpu as pltpu
from jax.sharding import PartitionSpec as P

BF16 = jnp.bfloat16
F32 = jnp.float32
MIB = 1024 * 1024
LINES = (((1,), (0,)), ((), ()))
ROWS = (((1,), (1,)), ((), ()))
COLS = (((0,), (0,)), ((), ()))
ANY = pl.BlockSpec(memory_space=pl.ANY)
ONCE = pl.Buffered(1)


def dot(x, y, dims=LINES):
    return lax.dot_general(x, y, dims, preferred_element_type=F32)


def params(limit=56):
    return pltpu.CompilerParams(vmem_limit_bytes=limit * MIB)


def cost(flops, moved):
    return pl.CostEstimate(flops=int(flops) // 16, bytes_accessed=int(moved) // 16, transcendentals=0)


def block_of(k):
    n_col, n_chan = lax.axis_size("col"), lax.axis_size("chan")
    col = lax.rem(lax.axis_index("col") + k // n_chan, n_col)
    return col * n_chan + lax.rem(lax.axis_index("chan") + k % n_chan, n_chan)


def order_kernel(env_ref, order_ref, left_ref, turned_ref):
    env = env_ref[...].reshape(order_ref.shape[0], env_ref.shape[2])
    left_ref[...] = dot(order_ref[...], env).astype(BF16)
    turned_ref[...] = dot(env, order_ref[...], (((0,), (1,)), ((), ()))).astype(BF16)


def ordered(env, tile):
    channels, bonds, depth = env.shape
    size = tile * channels
    index = jnp.arange(size)
    wanted = (index % channels) * tile + index // channels
    order = (wanted[:, None] == index[None, :]).astype(BF16)
    return pl.pallas_call(
        order_kernel,
        grid=(bonds // tile,),
        in_specs=[
            pl.BlockSpec((channels, tile, depth), lambda i: (0, i, 0)),
            pl.BlockSpec((size, size), lambda i: (0, 0)),
        ],
        out_specs=[
            pl.BlockSpec((size, depth), lambda i: (i, 0)),
            pl.BlockSpec((depth, size), lambda i: (0, i)),
        ],
        out_shape=[
            jax.ShapeDtypeStruct((bonds * channels, depth), BF16),
            jax.ShapeDtypeStruct((depth, bonds * channels), BF16),
        ],
        compiler_params=params(),
        cost_estimate=cost(4 * size * env.size, 6 * env.size),
    )(env, order)


def part_kernel(env_ref, *outs):
    lanes = outs[0].shape[1]
    for h, out in enumerate(outs):
        out[...] = env_ref[0, :, h * lanes : (h + 1) * lanes]


def parted(env, lanes):
    channels, far, width = env.shape
    count = width // lanes
    return pl.pallas_call(
        part_kernel,
        grid=(channels,),
        in_specs=[pl.BlockSpec((1, far, width), lambda v: (v, 0, 0))],
        out_specs=[pl.BlockSpec((far, lanes), lambda v: (0, v))] * count,
        out_shape=[jax.ShapeDtypeStruct((far, channels * lanes), BF16)] * count,
        compiler_params=params(),
        cost_estimate=cost(0, 4 * env.size),
    )(env)


def fore_kernel(channels, lanes, theta_ref, left_ref, mpo_ref, right_ref, *refs):
    out, ones, threes = refs[-3:]
    phys_pair = theta_ref.shape[1] // lanes
    pair, step = 2 * channels, 2 * phys_pair
    pairs = left_ref.shape[0] // pair
    full = dot(left_ref[...], theta_ref[...])
    for i in range(pairs):
        for s in range(0, phys_pair, 2):
            both = [
                full[i * pair : (i + 1) * pair, q * lanes : (q + 1) * lanes] for q in (s, s + 1)
            ]
            ones[s * pair : (s + 2) * pair, i * lanes : (i + 1) * lanes] = jnp.concatenate(
                both, axis=0
            ).astype(BF16)
    mixed = dot(mpo_ref[...], ones[...]).astype(BF16)
    for i in range(pairs):
        for v in range(channels):
            threes[i * step : (i + 1) * step, v * lanes : (v + 1) * lanes] = mixed[
                v * step : (v + 1) * step, i * lanes : (i + 1) * lanes
            ]
    part = dot(right_ref[...], threes[...], ROWS)
    if len(refs) == 4:
        part = part + refs[0][...]
    out[...] = part.astype(out.dtype)


def fore(theta, left, mpo, right, total, channels, group, groups, kind, tile):
    far = right.shape[0]
    lanes = right.shape[1] // channels
    phys_pair = theta.shape[1] // lanes
    bonds = left.shape[0] // channels // groups
    steps = bonds // tile
    totals = [] if total is None else [total]
    return pl.pallas_call(
        functools.partial(fore_kernel, channels, lanes),
        grid=(steps,),
        in_specs=[
            pl.BlockSpec(theta.shape, lambda i: (0, 0), pipeline_mode=ONCE),
            pl.BlockSpec((tile * channels, left.shape[1]), lambda i: (group * steps + i, 0)),
            pl.BlockSpec(mpo.shape, lambda i: (0, 0), pipeline_mode=ONCE),
            pl.BlockSpec(right.shape, lambda i: (0, 0), pipeline_mode=ONCE),
        ]
        + [pl.BlockSpec((far, tile * phys_pair), lambda i: (0, group * steps + i))] * len(totals),
        out_specs=pl.BlockSpec((far, tile * phys_pair), lambda i: (0, i)),
        out_shape=jax.ShapeDtypeStruct((far, bonds * phys_pair), kind),
        scratch_shapes=[
            pltpu.VMEM((2 * channels * phys_pair, tile // 2 * lanes), BF16),
            pltpu.VMEM((tile * phys_pair, channels * lanes), BF16),
        ],
        compiler_params=params(48),
        cost_estimate=cost(
            2 * bonds * phys_pair * right.shape[1] * (left.shape[1] + far)
            + bonds * mpo.size * lanes,
            2 * (theta.size + right.size + bonds * channels * left.shape[1])
            + 4 * far * bonds * phys_pair,
        ),
    )(theta, left, mpo, right, *totals)


def back_kernel(channels, n_parts, scattered, *refs):
    parts = refs[:n_parts]
    mpo_ref, right_ref = refs[n_parts : n_parts + 2]
    out_ref, joined, ones = refs[-3:]
    lanes = right_ref.shape[1] // channels
    phys_pair = out_ref.shape[1] // lanes
    pair, step = 2 * channels, 2 * phys_pair
    pairs = out_ref.shape[0] // pair
    height = parts[0].shape[0]
    for k, part in enumerate(parts):
        place = block_of(k) if scattered else k
        joined[pl.ds(pl.multiple_of(place * height, height), height), :] = part[...]
    full = dot(joined[...], right_ref[...], COLS).astype(BF16)
    for i in range(pairs):
        for v in range(channels):
            ones[v * step : (v + 1) * step, i * lanes : (i + 1) * lanes] = full[
                i * step : (i + 1) * step, v * lanes : (v + 1) * lanes
            ]
    mixed = dot(mpo_ref[...], ones[...])
    for i in range(0, pairs, 2):
        for s in range(phys_pair):
            both = [
                mixed[s * pair : (s + 1) * pair, j * lanes : (j + 1) * lanes] for j in (i, i + 1)
            ]
            out_ref[i * pair : (i + 2) * pair, s * lanes : (s + 1) * lanes] = jnp.concatenate(
                both, axis=0
            ).astype(BF16)


def back(parts, mpo, right, buffer, channels, phys_pair, group, groups, scattered, tile):
    columns = parts[0].shape[1]
    bonds = columns // phys_pair
    far = right.shape[0]
    lanes = right.shape[1] // channels
    steps = bonds // tile
    buffers = [] if buffer is None else [buffer]
    return pl.pallas_call(
        functools.partial(back_kernel, channels, len(parts), scattered),
        grid=(steps,),
        input_output_aliases={} if buffer is None else {len(parts) + 2: 0},
        in_specs=[pl.BlockSpec((p.shape[0], tile * phys_pair), lambda i: (0, i)) for p in parts]
        + [
            pl.BlockSpec(mpo.shape, lambda i: (0, 0), pipeline_mode=ONCE),
            pl.BlockSpec(right.shape, lambda i: (0, 0), pipeline_mode=ONCE),
        ]
        + [ANY] * len(buffers),
        out_specs=pl.BlockSpec(
            (tile * channels, phys_pair * lanes), lambda i: (group * steps + i, 0)
        ),
        out_shape=jax.ShapeDtypeStruct((groups * bonds * channels, phys_pair * lanes), BF16),
        scratch_shapes=[
            pltpu.VMEM((far, tile * phys_pair), BF16),
            pltpu.VMEM((2 * channels * phys_pair, tile // 2 * lanes), BF16),
        ],
        compiler_params=params(48),
        cost_estimate=cost(
            2 * right.size * columns + bonds * mpo.size * lanes,
            2 * (right.size + far * columns + bonds * channels * phys_pair * lanes),
        ),
    )(*parts, mpo, right, *buffers)


def last_kernel(left_ref, back_ref, out_ref):
    out_ref[...] = dot(left_ref[...], back_ref[...]).astype(BF16)


def last(left_t, backs, chunk, n_chunks):
    columns = backs.shape[1] // n_chunks
    steps = 2
    return pl.pallas_call(
        last_kernel,
        grid=(steps,),
        in_specs=[
            pl.BlockSpec(left_t.shape, lambda i: (0, 0), pipeline_mode=ONCE),
            pl.BlockSpec((backs.shape[0], columns // steps), lambda i: (0, chunk * steps + i)),
        ],
        out_specs=pl.BlockSpec((left_t.shape[0], columns // steps), lambda i: (0, i)),
        out_shape=jax.ShapeDtypeStruct((left_t.shape[0], columns), BF16),
        compiler_params=params(48),
        cost_estimate=cost(
            2 * left_t.size * columns,
            2 * (left_t.size + left_t.shape[1] * columns + left_t.shape[0] * columns),
        ),
    )(left_t, backs)


def after(arrays, *deps):
    return lax.optimization_barrier((arrays, deps))[0]


def shards(theta, left_env, right_env, mpo_left, mpo_right):
    bonds, channels, depth = left_env.shape
    rows, phys_pair, width = theta.shape
    scattered = lax.axis_size("col") == 2 and lax.axis_size("chan") == 2
    tile = min(32, bonds)
    lanes = min(128, width)
    halves = width // lanes
    groups = max(1, min(4, bonds // tile))
    swap = [(0, 1), (1, 0)]

    paired = jnp.einsum("wuxs,uvyt->wstxyv", mpo_left, mpo_right, precision=lax.Precision.HIGHEST)
    mpo = paired.reshape(channels, phys_pair, phys_pair, channels).astype(BF16)
    twice = jnp.einsum("wsxv,jk->sjwvkx", mpo, jnp.eye(2, dtype=BF16))
    size = 2 * channels * phys_pair
    mpo_back = twice.reshape(size, size)
    mpo_fore = mpo_back.T
    left, left_t = ordered(left_env.transpose(1, 0, 2), tile)
    right = parted(right_env.transpose(1, 0, 2), lanes)

    gathered = []
    for h in range(halves):
        piece = theta[:, :, h * lanes : (h + 1) * lanes].reshape(rows, phys_pair * lanes)
        if h > 0:
            piece = after(piece, gathered[-1], left, left_t, mpo_fore, mpo_back, right)
        gathered.append(lax.all_gather(piece, "row", axis=0, tiled=True))

    total = None
    for h in range(halves - 1):
        total = fore(gathered[h], left, mpo_fore, right[h], total, channels, 0, 1, F32, tile)

    def backward(h, g, parts, backs):
        return back(
            parts, mpo_back, right[h], backs, channels, phys_pair, g, groups, scattered, tile
        )

    own, everyone, backs = [], [], None
    block = gathered[-1]
    for g in range(groups):
        waits = own[g - 2 : g - 1] if g > 1 else []
        if g > 2:
            waits = waits + [everyone[g - 3][-1]]
        term = fore(
            after(block, *waits), left, mpo_fore, right[-1], total, channels, g, groups, BF16, tile
        )
        mine = lax.psum_scatter(term, ("col", "chan"), scatter_dimension=0, tiled=True)
        own.append(mine)
        if g > 1:
            backs = backward(0, g - 2, everyone[g - 2], backs)
            mine = after(mine, backs)
        if scattered:
            across = lax.ppermute(mine, "chan", swap)
            parts = [mine, across] + [lax.ppermute(p, "col", swap) for p in (mine, across)]
        else:
            parts = [lax.all_gather(mine, ("col", "chan"), axis=0, tiled=True)]
        everyone.append(parts)
    for g in range(max(groups - 2, 0), groups):
        backs = backward(0, g, everyone[g], backs)

    n_chunks = 2
    per = phys_pair // n_chunks
    products = []
    for h in range(halves):
        if h > 0:
            backs = None
            for g, parts in enumerate(everyone):
                waits = [term] if g < groups // 2 else products[-n_chunks : 1 - n_chunks]
                backs = backward(h, g, after(parts, *waits), backs)
        for c in range(n_chunks):
            if c > 0:
                backs = after(backs, term, *(products[-n_chunks : 1 - n_chunks] if h > 0 else []))
            term = last(left_t, backs, c, n_chunks)
            products.append(lax.psum_scatter(term, "row", scatter_dimension=0, tiled=True))
    products = [x.reshape(rows, per, lanes) for x in products]
    products = [
        jnp.concatenate(products[h * n_chunks : (h + 1) * n_chunks], axis=1) for h in range(halves)
    ]
    return jnp.concatenate(own, axis=1), jnp.concatenate(products, axis=2)


def solution(mesh):
    in_specs = (
        P(("grp", "row"), None, ("col", "chan")),
        P(("grp", "row"), None, None),
        P("grp", None, ("col", "chan")),
        P(),
        P(),
    )
    out_specs = (P(("grp", "col", "chan"), "row"), P(("grp", "row"), None, ("col", "chan")))
    return jax.shard_map(shards, mesh=mesh, in_specs=in_specs, out_specs=out_specs, check_vma=False)
```

```python
import functools

import jax
import jax.numpy as jnp
from jax import lax
from jax.experimental import pallas as pl
from jax.experimental.pallas import tpu as pltpu
from jax.sharding import PartitionSpec as P

BF16 = jnp.bfloat16
F32 = jnp.float32
MIB = 1024 * 1024
LINES = (((1,), (0,)), ((), ()))
ROWS = (((1,), (1,)), ((), ()))
COLS = (((0,), (0,)), ((), ()))
ANY = pl.BlockSpec(memory_space=pl.ANY)
ONCE = pl.Buffered(1)


def dot(x, y, dims=LINES):
    return lax.dot_general(x, y, dims, preferred_element_type=F32)


def params(limit=56):
    return pltpu.CompilerParams(vmem_limit_bytes=limit * MIB)


def cost(flops, moved):
    return pl.CostEstimate(flops=int(flops) // 16, bytes_accessed=int(moved) // 16, transcendentals=0)


def block_of(k):
    n_col, n_chan = lax.axis_size("col"), lax.axis_size("chan")
    col = lax.rem(lax.axis_index("col") + k // n_chan, n_col)
    return col * n_chan + lax.rem(lax.axis_index("chan") + k % n_chan, n_chan)


def order_kernel(env_ref, order_ref, left_ref, turned_ref):
    env = env_ref[...].reshape(order_ref.shape[0], env_ref.shape[2])
    left_ref[...] = dot(order_ref[...], env).astype(BF16)
    turned_ref[...] = dot(env, order_ref[...], (((0,), (1,)), ((), ()))).astype(BF16)


def ordered(env, tile):
    channels, bonds, depth = env.shape
    size = tile * channels
    index = jnp.arange(size)
    wanted = (index % channels) * tile + index // channels
    order = (wanted[:, None] == index[None, :]).astype(BF16)
    return pl.pallas_call(
        order_kernel,
        grid=(bonds // tile,),
        in_specs=[
            pl.BlockSpec((channels, tile, depth), lambda i: (0, i, 0)),
            pl.BlockSpec((size, size), lambda i: (0, 0)),
        ],
        out_specs=[
            pl.BlockSpec((size, depth), lambda i: (i, 0)),
            pl.BlockSpec((depth, size), lambda i: (0, i)),
        ],
        out_shape=[
            jax.ShapeDtypeStruct((bonds * channels, depth), BF16),
            jax.ShapeDtypeStruct((depth, bonds * channels), BF16),
        ],
        compiler_params=params(),
        cost_estimate=cost(4 * size * env.size, 6 * env.size),
    )(env, order)


def part_kernel(env_ref, *outs):
    lanes = outs[0].shape[1]
    for h, out in enumerate(outs):
        out[...] = env_ref[0, :, h * lanes : (h + 1) * lanes]


def parted(env, lanes):
    channels, far, width = env.shape
    count = width // lanes
    return pl.pallas_call(
        part_kernel,
        grid=(channels,),
        in_specs=[pl.BlockSpec((1, far, width), lambda v: (v, 0, 0))],
        out_specs=[pl.BlockSpec((far, lanes), lambda v: (0, v))] * count,
        out_shape=[jax.ShapeDtypeStruct((far, channels * lanes), BF16)] * count,
        compiler_params=params(),
        cost_estimate=cost(0, 4 * env.size),
    )(env)


def fore_kernel(channels, lanes, theta_ref, left_ref, mpo_ref, right_ref, *refs):
    out, ones, threes = refs[-3:]
    phys_pair = theta_ref.shape[1] // lanes
    pair, step = 2 * channels, 2 * phys_pair
    pairs = left_ref.shape[0] // pair
    full = dot(left_ref[...], theta_ref[...])
    for i in range(pairs):
        for s in range(0, phys_pair, 2):
            both = [
                full[i * pair : (i + 1) * pair, q * lanes : (q + 1) * lanes] for q in (s, s + 1)
            ]
            ones[s * pair : (s + 2) * pair, i * lanes : (i + 1) * lanes] = jnp.concatenate(
                both, axis=0
            ).astype(BF16)
    mixed = dot(mpo_ref[...], ones[...]).astype(BF16)
    for i in range(pairs):
        for v in range(channels):
            threes[i * step : (i + 1) * step, v * lanes : (v + 1) * lanes] = mixed[
                v * step : (v + 1) * step, i * lanes : (i + 1) * lanes
            ]
    part = dot(right_ref[...], threes[...], ROWS)
    if len(refs) == 4:
        part = part + refs[0][...]
    out[...] = part.astype(out.dtype)


def fore(theta, left, mpo, right, total, channels, group, groups, kind, tile, place=0):
    far = right.shape[0]
    lanes = right.shape[1] // channels
    phys_pair = theta.shape[1] // lanes
    bonds = left.shape[0] // channels // groups
    steps = bonds // tile
    totals = [] if total is None else [total]
    return pl.pallas_call(
        functools.partial(fore_kernel, channels, lanes),
        grid=(steps,),
        in_specs=[
            pl.BlockSpec(theta.shape, lambda i: (0, 0), pipeline_mode=ONCE),
            pl.BlockSpec((tile * channels, left.shape[1]), lambda i: (group * steps + i, 0)),
            pl.BlockSpec(mpo.shape, lambda i: (0, 0), pipeline_mode=ONCE),
            pl.BlockSpec(right.shape, lambda i: (0, 0), pipeline_mode=ONCE),
        ]
        + [pl.BlockSpec((far, tile * phys_pair), lambda i: (0, place * steps + i))] * len(totals),
        out_specs=pl.BlockSpec((far, tile * phys_pair), lambda i: (0, i)),
        out_shape=jax.ShapeDtypeStruct((far, bonds * phys_pair), kind),
        scratch_shapes=[
            pltpu.VMEM((2 * channels * phys_pair, tile // 2 * lanes), BF16),
            pltpu.VMEM((tile * phys_pair, channels * lanes), BF16),
        ],
        compiler_params=params(48),
        cost_estimate=cost(
            2 * bonds * phys_pair * right.shape[1] * (left.shape[1] + far)
            + bonds * mpo.size * lanes,
            2 * (theta.size + right.size + bonds * channels * left.shape[1])
            + 4 * far * bonds * phys_pair,
        ),
    )(theta, left, mpo, right, *totals)


def back_kernel(channels, n_parts, scattered, *refs):
    parts = refs[:n_parts]
    mpo_ref, right_ref = refs[n_parts : n_parts + 2]
    out_ref, joined, ones = refs[-3:]
    lanes = right_ref.shape[1] // channels
    phys_pair = out_ref.shape[1] // lanes
    pair, step = 2 * channels, 2 * phys_pair
    pairs = out_ref.shape[0] // pair
    height = parts[0].shape[0]
    for k, part in enumerate(parts):
        place = block_of(k) if scattered else k
        joined[pl.ds(pl.multiple_of(place * height, height), height), :] = part[...]
    full = dot(joined[...], right_ref[...], COLS).astype(BF16)
    for i in range(pairs):
        for v in range(channels):
            ones[v * step : (v + 1) * step, i * lanes : (i + 1) * lanes] = full[
                i * step : (i + 1) * step, v * lanes : (v + 1) * lanes
            ]
    mixed = dot(mpo_ref[...], ones[...])
    for i in range(0, pairs, 2):
        for s in range(phys_pair):
            both = [
                mixed[s * pair : (s + 1) * pair, j * lanes : (j + 1) * lanes] for j in (i, i + 1)
            ]
            out_ref[i * pair : (i + 2) * pair, s * lanes : (s + 1) * lanes] = jnp.concatenate(
                both, axis=0
            ).astype(BF16)


def back(parts, mpo, right, buffer, channels, phys_pair, group, groups, scattered, tile):
    columns = parts[0].shape[1]
    bonds = columns // phys_pair
    far = right.shape[0]
    lanes = right.shape[1] // channels
    steps = bonds // tile
    buffers = [] if buffer is None else [buffer]
    return pl.pallas_call(
        functools.partial(back_kernel, channels, len(parts), scattered),
        grid=(steps,),
        input_output_aliases={} if buffer is None else {len(parts) + 2: 0},
        in_specs=[pl.BlockSpec((p.shape[0], tile * phys_pair), lambda i: (0, i)) for p in parts]
        + [
            pl.BlockSpec(mpo.shape, lambda i: (0, 0), pipeline_mode=ONCE),
            pl.BlockSpec(right.shape, lambda i: (0, 0), pipeline_mode=ONCE),
        ]
        + [ANY] * len(buffers),
        out_specs=pl.BlockSpec(
            (tile * channels, phys_pair * lanes), lambda i: (group * steps + i, 0)
        ),
        out_shape=jax.ShapeDtypeStruct((groups * bonds * channels, phys_pair * lanes), BF16),
        scratch_shapes=[
            pltpu.VMEM((far, tile * phys_pair), BF16),
            pltpu.VMEM((2 * channels * phys_pair, tile // 2 * lanes), BF16),
        ],
        compiler_params=params(48),
        cost_estimate=cost(
            2 * right.size * columns + bonds * mpo.size * lanes,
            2 * (right.size + far * columns + bonds * channels * phys_pair * lanes),
        ),
    )(*parts, mpo, right, *buffers)


def last_kernel(left_ref, back_ref, out_ref):
    out_ref[...] = dot(left_ref[...], back_ref[...]).astype(BF16)


def last(left_t, backs, chunk, n_chunks):
    columns = backs.shape[1] // n_chunks
    steps = 2
    return pl.pallas_call(
        last_kernel,
        grid=(steps,),
        in_specs=[
            pl.BlockSpec(left_t.shape, lambda i: (0, 0), pipeline_mode=ONCE),
            pl.BlockSpec((backs.shape[0], columns // steps), lambda i: (0, chunk * steps + i)),
        ],
        out_specs=pl.BlockSpec((left_t.shape[0], columns // steps), lambda i: (0, i)),
        out_shape=jax.ShapeDtypeStruct((left_t.shape[0], columns), BF16),
        compiler_params=params(48),
        cost_estimate=cost(
            2 * left_t.size * columns,
            2 * (left_t.size + left_t.shape[1] * columns + left_t.shape[0] * columns),
        ),
    )(left_t, backs)


def join_kernel(n_rows, n_parts, *refs):
    blocks, out, sems = refs[:-2], refs[-2], refs[-1]
    depth, columns = blocks[0].shape
    reach = 2 * n_rows - 1
    for phase in ("start", "wait"):
        for k, block in enumerate(blocks):
            source = lax.axis_index("row") + (k % reach - (n_rows - 1))

            @pl.when((source >= 0) & (source < n_rows))
            def _():
                target = out.at[
                    pl.ds(pl.multiple_of(source * depth, depth), depth),
                    pl.ds(k // reach * columns, columns),
                ]
                getattr(pltpu.make_async_copy(block, target, sems.at[k]), phase)()


def join(parts, n_rows):
    blocks = [block for part in parts for block in part]
    depth, columns = blocks[0].shape
    return pl.pallas_call(
        functools.partial(join_kernel, n_rows, len(parts)),
        in_specs=[ANY] * len(blocks),
        out_specs=ANY,
        out_shape=jax.ShapeDtypeStruct((depth * n_rows, columns * len(parts)), BF16),
        scratch_shapes=[pltpu.SemaphoreType.DMA((len(blocks),))],
        cost_estimate=cost(0, 4 * depth * n_rows * columns * len(parts)),
    )(*blocks)


def after(arrays, *deps):
    return lax.optimization_barrier((arrays, deps))[0]


def gather_round(pair, t, n_rows):
    up = lax.ppermute(pair[0], "row", [(r, r + 1) for r in range(t - 1, n_rows - 1)])
    down = lax.ppermute(pair[1], "row", [(r, r - 1) for r in range(1, n_rows - t + 1)])
    return up, down


def row_block(term, distance, n_rows):
    height = term.shape[0] // n_rows
    block = lax.rem(lax.axis_index("row") + distance, n_rows)
    return lax.dynamic_slice_in_dim(term, block * height, height)


def scatter_inputs(term, pair, t, n_rows):
    up, down = row_block(term, n_rows - t, n_rows), row_block(term, t, n_rows)
    if pair is not None:
        up, down = add(up, pair[0]), add(down, pair[1])
    return lax.optimization_barrier((up, down))


def scatter_round(pair, t, n_rows):
    up = lax.ppermute(pair[0], "row", [(r, r + 1) for r in range(t)])
    down = lax.ppermute(pair[1], "row", [(n_rows - 1 - r, n_rows - 2 - r) for r in range(t)])
    return up, down


def add(x, y):
    return (x.astype(F32) + y.astype(F32)).astype(BF16)


def halved(term, axis):
    height = term.shape[0] // 2
    index = lax.axis_index(axis)
    return [lax.dynamic_slice_in_dim(term, k * height, height) for k in (index, 1 - index)]


def swapped(block, axis):
    return lax.ppermute(block, axis, [(0, 1), (1, 0)])


def shards(theta, left_env, right_env, mpo_left, mpo_right):
    bonds, channels, depth = left_env.shape
    rows, phys_pair, width = theta.shape
    n_rows = lax.axis_size("row")
    scattered = lax.axis_size("col") == 2 and lax.axis_size("chan") == 2
    tile = min(32, bonds)
    lanes = min(128, width)
    halves = width // lanes
    groups = max(1, min(4, bonds // tile))
    n_chunks = 2
    per = phys_pair // n_chunks

    paired = jnp.einsum("wuxs,uvyt->wstxyv", mpo_left, mpo_right, precision=lax.Precision.HIGHEST)
    mpo = paired.reshape(channels, phys_pair, phys_pair, channels).astype(BF16)
    twice = jnp.einsum("wsxv,jk->sjwvkx", mpo, jnp.eye(2, dtype=BF16))
    size = 2 * channels * phys_pair
    mpo_back = twice.reshape(size, size)
    mpo_fore = mpo_back.T
    left, left_t = ordered(left_env.transpose(1, 0, 2), tile)
    right = parted(right_env.transpose(1, 0, 2), lanes)

    theta_all, total, last_round = None, [None], [()] * n_chunks
    cuts = 2 if groups % 2 == 0 and n_rows > 2 else 1
    for h in range(halves):
        cut = theta[:, :, h * lanes : (h + 1) * lanes]
        pairs, blocks, fresh = [], [], []
        for c in range(n_chunks):
            piece = cut[:, c * per : (c + 1) * per].reshape(rows, per * lanes)
            pairs.append(after((piece, piece), *last_round[c]))
            blocks.append([piece])
        for t in range(1, n_rows):
            if h == 0 and t > 1:
                waits = [left, left_t] if t == 2 else [mpo_fore, mpo_back, right]
                pairs[0] = after(pairs[0], *waits)
            if h > 0 and t > 1 and len(fresh) < cuts:
                held = theta_all if t == 2 else after(theta_all, *pairs)
                fresh += [
                    fore(held, left, mpo_fore, right[h - 1], total[0], channels, len(fresh), cuts,
                         F32, tile)
                ]
                pairs = [after(pair, fresh[-1]) for pair in pairs]
            for c in range(n_chunks):
                pairs[c] = gather_round(pairs[c], t, n_rows)
                blocks[c] = [pairs[c][0]] + blocks[c] + [pairs[c][1]]
        while h > 0 and len(fresh) < cuts:
            fresh += [
                fore(theta_all, left, mpo_fore, right[h - 1], total[0], channels, len(fresh), cuts,
                     F32, tile)
            ]
        total = fresh or total
        last_round = pairs
        theta_all = join(blocks, n_rows)

    def forward(g, *deps):
        here = g * len(total) // groups
        return fore(
            after(theta_all, *deps), left, mpo_fore, right[-1], total[here], channels, g, groups,
            BF16, tile, g % (groups // len(total)),
        )

    def backward(h, g, parts, backs, *deps):
        parts = after(parts, *deps)
        return back(
            parts, mpo_back, right[h], backs, channels, phys_pair, g, groups, scattered, tile
        )

    terms, near, own, far, everyone, backs = [], [], [], [], [], None
    step = 0
    while len(everyone) < groups or step < 2 * groups:
        g = step - groups
        waits = []
        if scattered:
            for lag, done in ((2, near), (3, own), (4, far)):
                waits += done[step - lag : step - lag + 1] if step >= lag else []
        if step < groups:
            terms.append(forward(step, *waits))
            out = terms[-1]
        elif 0 <= g < len(everyone):
            backs = backward(0, g, everyone[g], backs, *waits)
            out = backs
        step += 1
        if not scattered:
            if step <= groups:
                own.append(lax.psum_scatter(out, ("col", "chan"), scatter_dimension=0, tiled=True))
                everyone.append([lax.all_gather(own[-1], ("col", "chan"), axis=0, tiled=True)])
            continue
        if len(everyone) < len(far):
            across = after(far[len(everyone)], out)
            pair = [own[len(everyone)], across]
            everyone.append(pair + [swapped(x, "col") for x in pair])
        if len(far) < len(own):
            far.append(swapped(after(own[len(far)], out), "chan"))
        if len(own) < len(near):
            mine, other = halved(after(near[len(own)], out), "chan")
            own.append(add(mine, swapped(other, "chan")))
        if len(near) < len(terms):
            mine, other = halved(terms[len(near)], "col")
            near.append(add(mine, swapped(other, "col")))
    for g in range(step - groups, groups):
        backs = backward(0, g, everyone[g], backs)

    terms, rounds = [], []

    def advance(i, *deps):
        t = len(rounds[i]) + 1
        if t < n_rows:
            pair = after(rounds[i][-1], *deps) if t > 1 else None
            ready = scatter_inputs(terms[i], pair, t, n_rows)
            rounds[i].append(scatter_round(ready, t, n_rows))
            return list(ready)

    def come(i, t):
        return list(rounds[i][min(t, len(rounds[i])) - 1])

    for h in range(halves):
        first = len(terms)
        if h > 0:
            one, two, backs = first - n_chunks, first - 1, None
            for g, parts in enumerate(everyone):
                waits = [terms[-1]] + come(one, 1) if g == 0 else []
                if g == 1:
                    waits = come(one, 2) + come(two, 1)
                    advance(one, backs)
                    advance(two, backs)
                elif g > 1 and g == groups - 1:
                    waits = come(one, 3) + come(two, 2)
                    advance(two, backs)
                backs = backward(h, g, parts, backs, *waits)
        for c in range(n_chunks):
            waits = come(first - 1, 3) if h > 0 and c > 0 else []
            waits += sent + terms[first:] if c > 0 else []
            terms.append(last(left_t, after(backs, *waits), c, n_chunks))
            rounds.append([])
            for i in range(first, len(terms)):
                sent = advance(i, terms[-1])
    products = []
    for i in range(len(terms)):
        while len(rounds[i]) < n_rows - 1:
            advance(i)
        total = row_block(terms[i], 0, n_rows).astype(F32)
        for x in rounds[i][-1]:
            total = total + x.astype(F32)
        products.append(total.astype(BF16).reshape(rows, per, lanes))
    products = [
        jnp.concatenate(products[h * n_chunks : (h + 1) * n_chunks], axis=1) for h in range(halves)
    ]
    return jnp.concatenate(own, axis=1), jnp.concatenate(products, axis=2)


def solution(mesh):
    in_specs = (
        P(("grp", "row"), None, ("col", "chan")),
        P(("grp", "row"), None, None),
        P("grp", None, ("col", "chan")),
        P(),
        P(),
    )
    out_specs = (P(("grp", "col", "chan"), "row"), P(("grp", "row"), None, ("col", "chan")))
    return jax.shard_map(shards, mesh=mesh, in_specs=in_specs, out_specs=out_specs, check_vma=False)
```

```python
import functools

import jax
import jax.numpy as jnp
from jax import lax
from jax.experimental import pallas as pl
from jax.experimental.pallas import tpu as pltpu
from jax.sharding import PartitionSpec as P

BF16 = jnp.bfloat16
F32 = jnp.float32
MIB = 1024 * 1024
LINES = (((1,), (0,)), ((), ()))
ROWS = (((1,), (1,)), ((), ()))
COLS = (((0,), (0,)), ((), ()))
ANY = pl.BlockSpec(memory_space=pl.ANY)
ONCE = pl.Buffered(1)


def dot(x, y, dims=LINES):
    return lax.dot_general(x, y, dims, preferred_element_type=F32)


def params(limit=56):
    return pltpu.CompilerParams(vmem_limit_bytes=limit * MIB)


def cost(flops, moved):
    return pl.CostEstimate(flops=int(flops) // 16, bytes_accessed=int(moved) // 16, transcendentals=0)


def block_of(k):
    n_col, n_chan = lax.axis_size("col"), lax.axis_size("chan")
    col = lax.rem(lax.axis_index("col") + k // n_chan, n_col)
    return col * n_chan + lax.rem(lax.axis_index("chan") + k % n_chan, n_chan)


def order_kernel(env_ref, order_ref, left_ref, turned_ref):
    env = env_ref[...].reshape(order_ref.shape[0], env_ref.shape[2])
    left_ref[...] = dot(order_ref[...], env).astype(BF16)
    turned_ref[...] = dot(env, order_ref[...], (((0,), (1,)), ((), ()))).astype(BF16)


def ordered(env, tile):
    channels, bonds, depth = env.shape
    size = tile * channels
    index = jnp.arange(size)
    wanted = (index % channels) * tile + index // channels
    order = (wanted[:, None] == index[None, :]).astype(BF16)
    return pl.pallas_call(
        order_kernel,
        grid=(bonds // tile,),
        in_specs=[
            pl.BlockSpec((channels, tile, depth), lambda i: (0, i, 0)),
            pl.BlockSpec((size, size), lambda i: (0, 0)),
        ],
        out_specs=[
            pl.BlockSpec((size, depth), lambda i: (i, 0)),
            pl.BlockSpec((depth, size), lambda i: (0, i)),
        ],
        out_shape=[
            jax.ShapeDtypeStruct((bonds * channels, depth), BF16),
            jax.ShapeDtypeStruct((depth, bonds * channels), BF16),
        ],
        compiler_params=params(),
        cost_estimate=cost(4 * size * env.size, 6 * env.size),
    )(env, order)


def part_kernel(env_ref, *outs):
    lanes = outs[0].shape[1]
    for h, out in enumerate(outs):
        out[...] = env_ref[0, :, h * lanes : (h + 1) * lanes]


def parted(env, lanes):
    channels, far, width = env.shape
    count = width // lanes
    return pl.pallas_call(
        part_kernel,
        grid=(channels,),
        in_specs=[pl.BlockSpec((1, far, width), lambda v: (v, 0, 0))],
        out_specs=[pl.BlockSpec((far, lanes), lambda v: (0, v))] * count,
        out_shape=[jax.ShapeDtypeStruct((far, channels * lanes), BF16)] * count,
        compiler_params=params(),
        cost_estimate=cost(0, 4 * env.size),
    )(env)


def fore_kernel(channels, lanes, theta_ref, left_ref, mpo_ref, right_ref, *refs):
    out, ones, threes = refs[-3:]
    phys_pair = theta_ref.shape[1] // lanes
    pair, step = 2 * channels, 2 * phys_pair
    pairs = left_ref.shape[0] // pair
    full = dot(left_ref[...], theta_ref[...])
    for i in range(pairs):
        for s in range(0, phys_pair, 2):
            both = [
                full[i * pair : (i + 1) * pair, q * lanes : (q + 1) * lanes] for q in (s, s + 1)
            ]
            ones[s * pair : (s + 2) * pair, i * lanes : (i + 1) * lanes] = jnp.concatenate(
                both, axis=0
            ).astype(BF16)
    mixed = dot(mpo_ref[...], ones[...]).astype(BF16)
    for i in range(pairs):
        for v in range(channels):
            threes[i * step : (i + 1) * step, v * lanes : (v + 1) * lanes] = mixed[
                v * step : (v + 1) * step, i * lanes : (i + 1) * lanes
            ]
    part = dot(right_ref[...], threes[...], ROWS)
    if len(refs) == 4:
        part = part + refs[0][...]
    out[...] = part.astype(out.dtype)


def fore(theta, left, mpo, right, total, channels, group, groups, kind, tile, place=0):
    far = right.shape[0]
    lanes = right.shape[1] // channels
    phys_pair = theta.shape[1] // lanes
    bonds = left.shape[0] // channels // groups
    steps = bonds // tile
    totals = [] if total is None else [total]
    return pl.pallas_call(
        functools.partial(fore_kernel, channels, lanes),
        grid=(steps,),
        in_specs=[
            pl.BlockSpec(theta.shape, lambda i: (0, 0), pipeline_mode=ONCE),
            pl.BlockSpec((tile * channels, left.shape[1]), lambda i: (group * steps + i, 0)),
            pl.BlockSpec(mpo.shape, lambda i: (0, 0), pipeline_mode=ONCE),
            pl.BlockSpec(right.shape, lambda i: (0, 0), pipeline_mode=ONCE),
        ]
        + [pl.BlockSpec((far, tile * phys_pair), lambda i: (0, place * steps + i))] * len(totals),
        out_specs=pl.BlockSpec((far, tile * phys_pair), lambda i: (0, i)),
        out_shape=jax.ShapeDtypeStruct((far, bonds * phys_pair), kind),
        scratch_shapes=[
            pltpu.VMEM((2 * channels * phys_pair, tile // 2 * lanes), BF16),
            pltpu.VMEM((tile * phys_pair, channels * lanes), BF16),
        ],
        compiler_params=params(48),
        cost_estimate=cost(
            2 * bonds * phys_pair * right.shape[1] * (left.shape[1] + far)
            + bonds * mpo.size * lanes,
            2 * (theta.size + right.size + bonds * channels * left.shape[1])
            + 4 * far * bonds * phys_pair,
        ),
    )(theta, left, mpo, right, *totals)


def back_kernel(channels, n_parts, n_halves, scattered, *refs):
    parts = refs[:n_parts]
    mpo_ref, rights = refs[n_parts], refs[n_parts + 1 : n_parts + 1 + n_halves]
    outs, joined, ones = refs[-2 - n_halves : -2], refs[-2], refs[-1]
    lanes = rights[0].shape[1] // channels
    phys_pair = outs[0].shape[1] // lanes
    pair, step = 2 * channels, 2 * phys_pair
    pairs = outs[0].shape[0] // pair
    height = parts[0].shape[0]
    for k, part in enumerate(parts):
        place = block_of(k) if scattered else k
        joined[pl.ds(pl.multiple_of(place * height, height), height), :] = part[...]
    for right_ref, out_ref in zip(rights, outs):
        full = dot(joined[...], right_ref[...], COLS).astype(BF16)
        for i in range(pairs):
            for v in range(channels):
                ones[v * step : (v + 1) * step, i * lanes : (i + 1) * lanes] = full[
                    i * step : (i + 1) * step, v * lanes : (v + 1) * lanes
                ]
        mixed = dot(mpo_ref[...], ones[...])
        for i in range(0, pairs, 2):
            for s in range(phys_pair):
                both = [
                    mixed[s * pair : (s + 1) * pair, j * lanes : (j + 1) * lanes]
                    for j in (i, i + 1)
                ]
                out_ref[i * pair : (i + 2) * pair, s * lanes : (s + 1) * lanes] = jnp.concatenate(
                    both, axis=0
                ).astype(BF16)


def back(parts, mpo, rights, buffers, channels, phys_pair, group, groups, scattered, tile):
    columns = parts[0].shape[1]
    bonds = columns // phys_pair
    far, width = rights[0].shape
    lanes = width // channels
    steps = bonds // tile
    count = len(rights)
    before = len(parts) + 1 + count
    return pl.pallas_call(
        functools.partial(back_kernel, channels, len(parts), count, scattered),
        grid=(steps,),
        input_output_aliases={before + k: k for k in range(len(buffers))},
        in_specs=[pl.BlockSpec((p.shape[0], tile * phys_pair), lambda i: (0, i)) for p in parts]
        + [pl.BlockSpec(mpo.shape, lambda i: (0, 0), pipeline_mode=ONCE)]
        + [pl.BlockSpec((far, width), lambda i: (0, 0), pipeline_mode=ONCE)] * count
        + [ANY] * len(buffers),
        out_specs=[
            pl.BlockSpec((tile * channels, phys_pair * lanes), lambda i: (group * steps + i, 0))
        ]
        * count,
        out_shape=[jax.ShapeDtypeStruct((groups * bonds * channels, phys_pair * lanes), BF16)]
        * count,
        scratch_shapes=[
            pltpu.VMEM((far, tile * phys_pair), BF16),
            pltpu.VMEM((2 * channels * phys_pair, tile // 2 * lanes), BF16),
        ],
        compiler_params=params(48),
        cost_estimate=cost(
            count * (2 * far * width * columns + bonds * mpo.size * lanes),
            2 * count * (far * width + bonds * channels * phys_pair * lanes) + 2 * far * columns,
        ),
    )(*parts, mpo, *rights, *buffers)


def last_kernel(left_ref, back_ref, out_ref):
    out_ref[...] = dot(left_ref[...], back_ref[...]).astype(BF16)


def last(left_t, backs, chunk, n_chunks):
    columns = backs.shape[1] // n_chunks
    steps = 2
    return pl.pallas_call(
        last_kernel,
        grid=(steps,),
        in_specs=[
            pl.BlockSpec(left_t.shape, lambda i: (0, 0), pipeline_mode=ONCE),
            pl.BlockSpec((backs.shape[0], columns // steps), lambda i: (0, chunk * steps + i)),
        ],
        out_specs=pl.BlockSpec((left_t.shape[0], columns // steps), lambda i: (0, i)),
        out_shape=jax.ShapeDtypeStruct((left_t.shape[0], columns), BF16),
        compiler_params=params(48),
        cost_estimate=cost(
            2 * left_t.size * columns,
            2 * (left_t.size + left_t.shape[1] * columns + left_t.shape[0] * columns),
        ),
    )(left_t, backs)


def join_kernel(n_rows, n_parts, *refs):
    blocks, out, sems = refs[:-2], refs[-2], refs[-1]
    depth, columns = blocks[0].shape
    reach = 2 * n_rows - 1
    for phase in ("start", "wait"):
        for k, block in enumerate(blocks):
            source = lax.axis_index("row") + (k % reach - (n_rows - 1))

            @pl.when((source >= 0) & (source < n_rows))
            def _():
                target = out.at[
                    pl.ds(pl.multiple_of(source * depth, depth), depth),
                    pl.ds(k // reach * columns, columns),
                ]
                getattr(pltpu.make_async_copy(block, target, sems.at[k]), phase)()


def join(parts, n_rows):
    blocks = [block for part in parts for block in part]
    depth, columns = blocks[0].shape
    return pl.pallas_call(
        functools.partial(join_kernel, n_rows, len(parts)),
        in_specs=[ANY] * len(blocks),
        out_specs=pl.BlockSpec(memory_space=pltpu.VMEM),
        out_shape=jax.ShapeDtypeStruct((depth * n_rows, columns * len(parts)), BF16),
        scratch_shapes=[pltpu.SemaphoreType.DMA((len(blocks),))],
        compiler_params=params(16),
        cost_estimate=cost(0, 4 * depth * n_rows * columns * len(parts)),
    )(*blocks)


def after(arrays, *deps):
    return lax.optimization_barrier((arrays, deps))[0]


def gather_round(pair, t, n_rows):
    up = lax.ppermute(pair[0], "row", [(r, r + 1) for r in range(t - 1, n_rows - 1)])
    down = lax.ppermute(pair[1], "row", [(r, r - 1) for r in range(1, n_rows - t + 1)])
    return up, down


def row_block(term, distance, n_rows):
    height = term.shape[0] // n_rows
    block = lax.rem(lax.axis_index("row") + distance, n_rows)
    return lax.dynamic_slice_in_dim(term, block * height, height)


def scatter_inputs(term, pair, t, n_rows):
    up, down = row_block(term, n_rows - t, n_rows), row_block(term, t, n_rows)
    if pair is not None:
        up, down = add(up, pair[0]), add(down, pair[1])
    return lax.optimization_barrier((up, down))


def scatter_round(pair, t, n_rows):
    up = lax.ppermute(pair[0], "row", [(r, r + 1) for r in range(t)])
    down = lax.ppermute(pair[1], "row", [(n_rows - 1 - r, n_rows - 2 - r) for r in range(t)])
    return up, down


def add(x, y):
    return (x.astype(F32) + y.astype(F32)).astype(BF16)


def halved(term, axis):
    height = term.shape[0] // 2
    index = lax.axis_index(axis)
    return [lax.dynamic_slice_in_dim(term, k * height, height) for k in (index, 1 - index)]


def swapped(block, axis):
    return lax.ppermute(block, axis, [(0, 1), (1, 0)])


def shards(theta, left_env, right_env, mpo_left, mpo_right):
    bonds, channels, depth = left_env.shape
    rows, phys_pair, width = theta.shape
    n_rows = lax.axis_size("row")
    scattered = lax.axis_size("col") == 2 and lax.axis_size("chan") == 2
    tile = min(32, bonds)
    lanes = min(128, width)
    halves = width // lanes
    groups = max(1, min(4, bonds // tile))
    n_chunks = 2
    per = phys_pair // n_chunks

    paired = jnp.einsum("wuxs,uvyt->wstxyv", mpo_left, mpo_right, precision=lax.Precision.HIGHEST)
    mpo = paired.reshape(channels, phys_pair, phys_pair, channels).astype(BF16)
    twice = jnp.einsum("wsxv,jk->sjwvkx", mpo, jnp.eye(2, dtype=BF16))
    size = 2 * channels * phys_pair
    mpo_back = twice.reshape(size, size)
    mpo_fore = mpo_back.T
    left, left_t = ordered(left_env.transpose(1, 0, 2), tile)
    right = parted(right_env.transpose(1, 0, 2), lanes)

    theta_all, total, last_round = None, [None], [()] * n_chunks
    cuts = 2 if groups % 2 == 0 and n_rows > 2 else 1
    for h in range(halves):
        cut = theta[:, :, h * lanes : (h + 1) * lanes]
        pairs, blocks, fresh = [], [], []
        for c in range(n_chunks):
            piece = cut[:, c * per : (c + 1) * per].reshape(rows, per * lanes)
            pairs.append(after((piece, piece), *last_round[c]))
            blocks.append([piece])
        for t in range(1, n_rows):
            if (h, t) == (0, 2):
                pairs[0] = after(pairs[0], left, left_t)
            if (h, t) == (1, 1):
                pairs[0] = after(pairs[0], mpo_fore, mpo_back, right)
            if h > 0 and t > 1 and len(fresh) < cuts:
                held = theta_all if t == 2 else after(theta_all, *sent)
                fresh += [
                    fore(held, left, mpo_fore, right[h - 1], total[0], channels, len(fresh), cuts,
                         F32, tile)
                ]
                pairs = [after(pair, fresh[-1]) for pair in pairs]
            sent = list(pairs)
            for c in range(n_chunks):
                pairs[c] = gather_round(pairs[c], t, n_rows)
                blocks[c] = [pairs[c][0]] + blocks[c] + [pairs[c][1]]
        while h > 0 and len(fresh) < cuts:
            fresh += [
                fore(theta_all, left, mpo_fore, right[h - 1], total[0], channels, len(fresh), cuts,
                     F32, tile)
            ]
        total = fresh or total
        last_round = pairs
        theta_all = join(blocks, n_rows)

    def forward(g, *deps):
        here = g * len(total) // groups
        return fore(
            after(theta_all, *deps), left, mpo_fore, right[-1], total[here], channels, g, groups,
            BF16, tile, g % (groups // len(total)),
        )

    def backward(g, backs, *deps):
        parts = after(everyone[g], *deps)
        return back(parts, mpo_back, right, backs, channels, phys_pair, g, groups, scattered, tile)

    terms, near, own, far, everyone, backs = [], [], [], [], [], []
    step = 0
    while len(everyone) < groups or step < 2 * groups:
        g = step - groups
        waits = []
        if scattered:
            for lag, done in ((2, near), (3, own), (4, far)):
                waits += done[step - lag : step - lag + 1] if step >= lag else []
        if step < groups:
            terms.append(forward(step, *waits))
            out = terms[-1]
        elif 0 <= g < len(everyone):
            backs = backward(g, backs, *waits)
            out = backs[-1]
        step += 1
        if not scattered:
            if step <= groups:
                own.append(lax.psum_scatter(out, ("col", "chan"), scatter_dimension=0, tiled=True))
                everyone.append([lax.all_gather(own[-1], ("col", "chan"), axis=0, tiled=True)])
            continue
        if len(everyone) < len(far):
            across = after(far[len(everyone)], out)
            pair = [own[len(everyone)], across]
            everyone.append(pair + [swapped(x, "col") for x in pair])
        if len(far) < len(own):
            far.append(swapped(after(own[len(far)], out), "chan"))
        if len(own) < len(near):
            mine, other = halved(after(near[len(own)], out), "chan")
            own.append(add(mine, swapped(other, "chan")))
        if len(near) < len(terms):
            mine, other = halved(terms[len(near)], "col")
            near.append(add(mine, swapped(other, "col")))
    for g in range(step - groups, groups):
        backs = backward(g, backs)

    terms, rounds = [], []

    def advance(i, *deps):
        t = len(rounds[i]) + 1
        if t < n_rows:
            pair = after(rounds[i][-1], *deps) if t > 1 else None
            ready = scatter_inputs(terms[i], pair, t, n_rows)
            rounds[i].append(scatter_round(ready, t, n_rows))
            return list(ready)

    def come(i, t):
        return list(rounds[i][min(t, len(rounds[i])) - 1])

    for i in range(halves * n_chunks):
        waits = sent + terms[-1:] if i > 0 else []
        waits += come(i - 2, 1) if i > 1 else []
        waits += come(i - 3, 2) if i > 2 else []
        terms.append(last(left_t, after(backs[i // n_chunks], *waits), i % n_chunks, n_chunks))
        rounds.append([])
        for j in range(i + 1):
            sent = advance(j, terms[-1])
    products = []
    for i in range(len(terms)):
        while len(rounds[i]) < n_rows - 1:
            advance(i)
        total = row_block(terms[i], 0, n_rows).astype(F32)
        for x in rounds[i][-1]:
            total = total + x.astype(F32)
        products.append(total.astype(BF16).reshape(rows, per, lanes))
    products = [
        jnp.concatenate(products[h * n_chunks : (h + 1) * n_chunks], axis=1) for h in range(halves)
    ]
    return jnp.concatenate(own, axis=1), jnp.concatenate(products, axis=2)


def solution(mesh):
    in_specs = (
        P(("grp", "row"), None, ("col", "chan")),
        P(("grp", "row"), None, None),
        P("grp", None, ("col", "chan")),
        P(),
        P(),
    )
    out_specs = (P(("grp", "col", "chan"), "row"), P(("grp", "row"), None, ("col", "chan")))
    return jax.shard_map(shards, mesh=mesh, in_specs=in_specs, out_specs=out_specs, check_vma=False)
```

```python
import functools

import jax
import jax.numpy as jnp
from jax import lax
from jax.experimental import pallas as pl
from jax.experimental.pallas import tpu as pltpu
from jax.sharding import PartitionSpec as P

BF16 = jnp.bfloat16
F32 = jnp.float32
MIB = 1024 * 1024
LINES = (((1,), (0,)), ((), ()))
ROWS = (((1,), (1,)), ((), ()))
COLS = (((0,), (0,)), ((), ()))
ANY = pl.BlockSpec(memory_space=pl.ANY)
ONCE = pl.Buffered(1)


def dot(x, y, dims=LINES):
    return lax.dot_general(x, y, dims, preferred_element_type=F32)


def params(limit=56):
    return pltpu.CompilerParams(vmem_limit_bytes=limit * MIB)


def cost(flops, moved):
    return pl.CostEstimate(flops=int(flops) // 16, bytes_accessed=int(moved) // 16, transcendentals=0)


def block_of(k):
    n_col, n_chan = lax.axis_size("col"), lax.axis_size("chan")
    col = lax.rem(lax.axis_index("col") + k // n_chan, n_col)
    return col * n_chan + lax.rem(lax.axis_index("chan") + k % n_chan, n_chan)


def order_kernel(env_ref, order_ref, left_ref, turned_ref):
    env = env_ref[...].reshape(order_ref.shape[0], env_ref.shape[2])
    left_ref[...] = dot(order_ref[...], env).astype(BF16)
    turned_ref[...] = dot(env, order_ref[...], (((0,), (1,)), ((), ()))).astype(BF16)


def ordered(env, tile):
    channels, bonds, depth = env.shape
    size = tile * channels
    index = jnp.arange(size)
    wanted = (index % channels) * tile + index // channels
    order = (wanted[:, None] == index[None, :]).astype(BF16)
    return pl.pallas_call(
        order_kernel,
        grid=(bonds // tile,),
        in_specs=[
            pl.BlockSpec((channels, tile, depth), lambda i: (0, i, 0)),
            pl.BlockSpec((size, size), lambda i: (0, 0)),
        ],
        out_specs=[
            pl.BlockSpec((size, depth), lambda i: (i, 0)),
            pl.BlockSpec((depth, size), lambda i: (0, i)),
        ],
        out_shape=[
            jax.ShapeDtypeStruct((bonds * channels, depth), BF16),
            jax.ShapeDtypeStruct((depth, bonds * channels), BF16),
        ],
        compiler_params=params(),
        cost_estimate=cost(4 * size * env.size, 6 * env.size),
    )(env, order)


def part_kernel(env_ref, *outs):
    lanes = outs[0].shape[1]
    for h, out in enumerate(outs):
        out[...] = env_ref[0, :, h * lanes : (h + 1) * lanes]


def parted(env, lanes):
    channels, far, width = env.shape
    count = width // lanes
    return pl.pallas_call(
        part_kernel,
        grid=(channels,),
        in_specs=[pl.BlockSpec((1, far, width), lambda v: (v, 0, 0))],
        out_specs=[pl.BlockSpec((far, lanes), lambda v: (0, v))] * count,
        out_shape=[jax.ShapeDtypeStruct((far, channels * lanes), BF16)] * count,
        compiler_params=params(),
        cost_estimate=cost(0, 4 * env.size),
    )(env)


def fore_kernel(channels, lanes, theta_ref, left_ref, mpo_ref, right_ref, *refs):
    out, ones, threes = refs[-3:]
    phys_pair = theta_ref.shape[1] // lanes
    pair, step = 2 * channels, 2 * phys_pair
    pairs = left_ref.shape[0] // pair
    full = dot(left_ref[...], theta_ref[...])
    for i in range(pairs):
        for s in range(0, phys_pair, 2):
            both = [
                full[i * pair : (i + 1) * pair, q * lanes : (q + 1) * lanes] for q in (s, s + 1)
            ]
            ones[s * pair : (s + 2) * pair, i * lanes : (i + 1) * lanes] = jnp.concatenate(
                both, axis=0
            ).astype(BF16)
    mixed = dot(mpo_ref[...], ones[...]).astype(BF16)
    for i in range(pairs):
        for v in range(channels):
            threes[i * step : (i + 1) * step, v * lanes : (v + 1) * lanes] = mixed[
                v * step : (v + 1) * step, i * lanes : (i + 1) * lanes
            ]
    part = dot(right_ref[...], threes[...], ROWS)
    if len(refs) == 4:
        part = part + refs[0][...]
    out[...] = part.astype(out.dtype)


def fore(theta, left, mpo, right, total, channels, group, groups, kind, tile, place=0):
    far = right.shape[0]
    lanes = right.shape[1] // channels
    phys_pair = theta.shape[1] // lanes
    bonds = left.shape[0] // channels // groups
    steps = bonds // tile
    totals = [] if total is None else [total]
    return pl.pallas_call(
        functools.partial(fore_kernel, channels, lanes),
        grid=(steps,),
        in_specs=[
            pl.BlockSpec(theta.shape, lambda i: (0, 0), pipeline_mode=ONCE),
            pl.BlockSpec((tile * channels, left.shape[1]), lambda i: (group * steps + i, 0)),
            pl.BlockSpec(mpo.shape, lambda i: (0, 0), pipeline_mode=ONCE),
            pl.BlockSpec(right.shape, lambda i: (0, 0), pipeline_mode=ONCE),
        ]
        + [pl.BlockSpec((far, tile * phys_pair), lambda i: (0, place * steps + i))] * len(totals),
        out_specs=pl.BlockSpec((far, tile * phys_pair), lambda i: (0, i)),
        out_shape=jax.ShapeDtypeStruct((far, bonds * phys_pair), kind),
        scratch_shapes=[
            pltpu.VMEM((2 * channels * phys_pair, tile // 2 * lanes), BF16),
            pltpu.VMEM((tile * phys_pair, channels * lanes), BF16),
        ],
        compiler_params=params(48),
        cost_estimate=cost(
            2 * bonds * phys_pair * right.shape[1] * (left.shape[1] + far)
            + bonds * mpo.size * lanes,
            2 * (theta.size + right.size + bonds * channels * left.shape[1])
            + 4 * far * bonds * phys_pair,
        ),
    )(theta, left, mpo, right, *totals)


def back_kernel(channels, n_parts, n_halves, scattered, *refs):
    parts = refs[:n_parts]
    mpo_ref, rights = refs[n_parts], refs[n_parts + 1 : n_parts + 1 + n_halves]
    outs, joined, ones = refs[-2 - n_halves : -2], refs[-2], refs[-1]
    lanes = rights[0].shape[1] // channels
    phys_pair = outs[0].shape[1] // lanes
    pair, step = 2 * channels, 2 * phys_pair
    pairs = outs[0].shape[0] // pair
    height = parts[0].shape[0]
    for k, part in enumerate(parts):
        place = block_of(k) if scattered else k
        joined[pl.ds(pl.multiple_of(place * height, height), height), :] = part[...]
    for right_ref, out_ref in zip(rights, outs):
        full = dot(joined[...], right_ref[...], COLS).astype(BF16)
        for i in range(pairs):
            for v in range(channels):
                ones[v * step : (v + 1) * step, i * lanes : (i + 1) * lanes] = full[
                    i * step : (i + 1) * step, v * lanes : (v + 1) * lanes
                ]
        mixed = dot(mpo_ref[...], ones[...])
        for i in range(0, pairs, 2):
            for s in range(phys_pair):
                both = [
                    mixed[s * pair : (s + 1) * pair, j * lanes : (j + 1) * lanes]
                    for j in (i, i + 1)
                ]
                out_ref[i * pair : (i + 2) * pair, s * lanes : (s + 1) * lanes] = jnp.concatenate(
                    both, axis=0
                ).astype(BF16)


def back(parts, mpo, rights, buffers, channels, phys_pair, group, groups, scattered, tile):
    columns = parts[0].shape[1]
    bonds = columns // phys_pair
    far, width = rights[0].shape
    lanes = width // channels
    steps = bonds // tile
    count = len(rights)
    before = len(parts) + 1 + count
    return pl.pallas_call(
        functools.partial(back_kernel, channels, len(parts), count, scattered),
        grid=(steps,),
        input_output_aliases={before + k: k for k in range(len(buffers))},
        in_specs=[pl.BlockSpec((p.shape[0], tile * phys_pair), lambda i: (0, i)) for p in parts]
        + [pl.BlockSpec(mpo.shape, lambda i: (0, 0), pipeline_mode=ONCE)]
        + [pl.BlockSpec((far, width), lambda i: (0, 0), pipeline_mode=ONCE)] * count
        + [ANY] * len(buffers),
        out_specs=[
            pl.BlockSpec((tile * channels, phys_pair * lanes), lambda i: (group * steps + i, 0))
        ]
        * count,
        out_shape=[jax.ShapeDtypeStruct((groups * bonds * channels, phys_pair * lanes), BF16)]
        * count,
        scratch_shapes=[
            pltpu.VMEM((far, tile * phys_pair), BF16),
            pltpu.VMEM((2 * channels * phys_pair, tile // 2 * lanes), BF16),
        ],
        compiler_params=params(48),
        cost_estimate=cost(
            count * (2 * far * width * columns + bonds * mpo.size * lanes),
            2 * count * (far * width + bonds * channels * phys_pair * lanes) + 2 * far * columns,
        ),
    )(*parts, mpo, *rights, *buffers)


def last_kernel(left_ref, back_ref, out_ref):
    out_ref[...] = dot(left_ref[...], back_ref[...]).astype(BF16)


def last(left_t, backs, chunk, n_chunks):
    columns = backs.shape[1] // n_chunks
    steps = 2
    return pl.pallas_call(
        last_kernel,
        grid=(steps,),
        in_specs=[
            pl.BlockSpec(left_t.shape, lambda i: (0, 0), pipeline_mode=ONCE),
            pl.BlockSpec((backs.shape[0], columns // steps), lambda i: (0, chunk * steps + i)),
        ],
        out_specs=pl.BlockSpec((left_t.shape[0], columns // steps), lambda i: (0, i)),
        out_shape=jax.ShapeDtypeStruct((left_t.shape[0], columns), BF16),
        compiler_params=params(48),
        cost_estimate=cost(
            2 * left_t.size * columns,
            2 * (left_t.size + left_t.shape[1] * columns + left_t.shape[0] * columns),
        ),
    )(left_t, backs)


def join_kernel(n_rows, n_parts, *refs):
    blocks, out, sems = refs[:-2], refs[-2], refs[-1]
    depth, columns = blocks[0].shape
    reach = 2 * n_rows - 1
    for phase in ("start", "wait"):
        for k, block in enumerate(blocks):
            source = lax.axis_index("row") + (k % reach - (n_rows - 1))

            @pl.when((source >= 0) & (source < n_rows))
            def _():
                target = out.at[
                    pl.ds(pl.multiple_of(source * depth, depth), depth),
                    pl.ds(k // reach * columns, columns),
                ]
                getattr(pltpu.make_async_copy(block, target, sems.at[k]), phase)()


def join(parts, n_rows):
    blocks = [block for part in parts for block in part]
    depth, columns = blocks[0].shape
    return pl.pallas_call(
        functools.partial(join_kernel, n_rows, len(parts)),
        in_specs=[ANY] * len(blocks),
        out_specs=pl.BlockSpec(memory_space=pltpu.VMEM),
        out_shape=jax.ShapeDtypeStruct((depth * n_rows, columns * len(parts)), BF16),
        scratch_shapes=[pltpu.SemaphoreType.DMA((len(blocks),))],
        compiler_params=params(),
        cost_estimate=cost(0, 4 * depth * n_rows * columns * len(parts)),
    )(*blocks)


def after(arrays, *deps):
    return lax.optimization_barrier((arrays, deps))[0]


def gather_round(pair, t, n_rows):
    up = lax.ppermute(pair[0], "row", [(r, r + 1) for r in range(t - 1, n_rows - 1)])
    down = lax.ppermute(pair[1], "row", [(r, r - 1) for r in range(1, n_rows - t + 1)])
    return up, down


def row_block(term, distance, n_rows):
    height = term.shape[0] // n_rows
    block = lax.rem(lax.axis_index("row") + distance, n_rows)
    return lax.dynamic_slice_in_dim(term, block * height, height)


def scatter_inputs(term, pair, t, n_rows):
    up, down = row_block(term, n_rows - t, n_rows), row_block(term, t, n_rows)
    if pair is not None:
        up, down = add(up, pair[0]), add(down, pair[1])
    return lax.optimization_barrier((up, down))


def scatter_round(pair, t, n_rows):
    up = lax.ppermute(pair[0], "row", [(r, r + 1) for r in range(t)])
    down = lax.ppermute(pair[1], "row", [(n_rows - 1 - r, n_rows - 2 - r) for r in range(t)])
    return up, down


def add(x, y):
    return (x.astype(F32) + y.astype(F32)).astype(BF16)


def halved(term, axis):
    height = term.shape[0] // 2
    index = lax.axis_index(axis)
    return [lax.dynamic_slice_in_dim(term, k * height, height) for k in (index, 1 - index)]


def swapped(block, axis):
    return lax.ppermute(block, axis, [(0, 1), (1, 0)])


def shards(theta, left_env, right_env, mpo_left, mpo_right):
    bonds, channels, depth = left_env.shape
    rows, phys_pair, width = theta.shape
    n_rows = lax.axis_size("row")
    scattered = lax.axis_size("col") == 2 and lax.axis_size("chan") == 2
    tile = min(32, bonds)
    lanes = min(128, width)
    halves = width // lanes
    groups = max(1, min(4, bonds // tile))
    n_chunks = 2
    per = phys_pair // n_chunks

    def environments(*deps):
        own_left, own_right, far_env = after((mpo_left, mpo_right, right_env), *deps)
        paired = jnp.einsum("wuxs,uvyt->wstxyv", own_left, own_right, precision=lax.Precision.HIGHEST)
        mpo = paired.reshape(channels, phys_pair, phys_pair, channels).astype(BF16)
        twice = jnp.einsum("wsxv,jk->sjwvkx", mpo, jnp.eye(2, dtype=BF16))
        size = 2 * channels * phys_pair
        mpo_back = twice.reshape(size, size)
        return mpo_back.T, mpo_back, parted(far_env.transpose(1, 0, 2), lanes)

    left, left_t = ordered(left_env.transpose(1, 0, 2), tile)
    if halves == 1:
        mpo_fore, mpo_back, right = environments()

    theta_all, total, last_round = None, [None], [()] * n_chunks
    cuts = 2 if groups % 2 == 0 and n_rows > 2 else 1
    for h in range(halves):
        cut = theta[:, :, h * lanes : (h + 1) * lanes]
        pairs, blocks, fresh = [], [], []

        def ahead(*deps):
            return [
                fore(
                    after(theta_all, *deps, *fresh), left, mpo_fore, right[h - 1], total[0], channels,
                    len(fresh), cuts, F32, tile,
                )
            ]

        for c in range(n_chunks):
            piece = cut[:, c * per : (c + 1) * per].reshape(rows, per * lanes)
            pairs.append(after((piece, piece), *last_round[c]))
            blocks.append([piece])
        for t in range(1, n_rows):
            came = list(pairs)
            if (h, t) == (0, 2):
                pairs[0] = after(pairs[0], left, left_t)
            if (h, t) == (1, 2):
                pairs = [after(pair, mpo_fore, mpo_back, right) for pair in pairs]
            if h > 0 and t > 2 and len(fresh) < cuts:
                fresh += ahead(*sent)
                pairs = [after(pair, fresh[-1]) for pair in pairs]
            sent = came
            for c in range(n_chunks):
                pairs[c] = gather_round(pairs[c], t, n_rows)
                blocks[c] = [pairs[c][0]] + blocks[c] + [pairs[c][1]]
        while h > 0 and len(fresh) < cuts:
            fresh += ahead(*sent)
        total = fresh or total
        last_round = pairs
        if h == 0 and halves > 1:
            mpo_fore, mpo_back, right = environments(*pairs)
        theta_all = join(after(blocks, *fresh), n_rows)

    def forward(g, *deps):
        here = g * len(total) // groups
        return fore(
            after(theta_all, *deps), left, mpo_fore, right[-1], total[here], channels, g, groups,
            BF16, tile, g % (groups // len(total)),
        )

    def backward(g, backs, *deps):
        parts = after(everyone[g], *deps)
        return back(parts, mpo_back, right, backs, channels, phys_pair, g, groups, scattered, tile)

    terms, near, own, far, everyone, backs = [], [], [], [], [], []
    step = 0
    while len(everyone) < groups or step < 2 * groups:
        g = step - groups
        waits = []
        if scattered:
            for lag, done in ((2, near), (3, own), (4, far)):
                waits += done[step - lag : step - lag + 1] if step >= lag else []
        if step < groups:
            terms.append(forward(step, *waits))
            out = terms[-1]
        elif 0 <= g < len(everyone):
            backs = backward(g, backs, *waits)
            out = backs[-1]
        step += 1
        if not scattered:
            if step <= groups:
                own.append(lax.psum_scatter(out, ("col", "chan"), scatter_dimension=0, tiled=True))
                everyone.append([lax.all_gather(own[-1], ("col", "chan"), axis=0, tiled=True)])
            continue
        if len(everyone) < len(far):
            across = after(far[len(everyone)], out)
            pair = [own[len(everyone)], across]
            everyone.append(pair + [swapped(x, "col") for x in pair])
        if len(far) < len(own):
            far.append(swapped(after(own[len(far)], out), "chan"))
        if len(own) < len(near):
            mine, other = halved(after(near[len(own)], out), "chan")
            own.append(add(mine, swapped(other, "chan")))
        if len(near) < len(terms):
            mine, other = halved(terms[len(near)], "col")
            near.append(add(mine, swapped(other, "col")))
    for g in range(step - groups, groups):
        backs = backward(g, backs)

    terms, rounds = [], []

    def advance(i, *deps):
        t = len(rounds[i]) + 1
        if t < n_rows:
            pair = after(rounds[i][-1], *deps) if t > 1 else None
            ready = scatter_inputs(terms[i], pair, t, n_rows)
            rounds[i].append(scatter_round(ready, t, n_rows))
            return list(ready)

    def come(i, t):
        return list(rounds[i][min(t, len(rounds[i])) - 1])

    for i in range(halves * n_chunks):
        waits = sent + terms[-1:] if i > 0 else []
        waits += come(i - 2, 1) if i > 1 else []
        waits += come(i - 3, 2) if i > 2 else []
        terms.append(last(left_t, after(backs[i // n_chunks], *waits), i % n_chunks, n_chunks))
        rounds.append([])
        for j in range(i + 1):
            sent = advance(j, terms[-1])
    products = []
    for i in range(len(terms)):
        while len(rounds[i]) < n_rows - 1:
            advance(i)
        total = row_block(terms[i], 0, n_rows).astype(F32)
        for x in rounds[i][-1]:
            total = total + x.astype(F32)
        products.append(total.astype(BF16).reshape(rows, per, lanes))
    products = [
        jnp.concatenate(products[h * n_chunks : (h + 1) * n_chunks], axis=1) for h in range(halves)
    ]
    return jnp.concatenate(own, axis=1), jnp.concatenate(products, axis=2)


def solution(mesh):
    in_specs = (
        P(("grp", "row"), None, ("col", "chan")),
        P(("grp", "row"), None, None),
        P("grp", None, ("col", "chan")),
        P(),
        P(),
    )
    out_specs = (P(("grp", "col", "chan"), "row"), P(("grp", "row"), None, ("col", "chan")))
    return jax.shard_map(shards, mesh=mesh, in_specs=in_specs, out_specs=out_specs, check_vma=False)
```

```python
import functools

import jax
import jax.numpy as jnp
from jax import lax
from jax.experimental import pallas as pl
from jax.experimental.pallas import tpu as pltpu
from jax.sharding import PartitionSpec as P

BF16 = jnp.bfloat16
F32 = jnp.float32
MIB = 1024 * 1024
LINES = (((1,), (0,)), ((), ()))
ROWS = (((1,), (1,)), ((), ()))
COLS = (((0,), (0,)), ((), ()))
ANY = pl.BlockSpec(memory_space=pl.ANY)
ONCE = pl.Buffered(1)


def dot(x, y, dims=LINES):
    return lax.dot_general(x, y, dims, preferred_element_type=F32)


def params(limit=56):
    return pltpu.CompilerParams(vmem_limit_bytes=limit * MIB)


def cost(flops, moved):
    return pl.CostEstimate(flops=int(flops) // 16, bytes_accessed=int(moved) // 16, transcendentals=0)


def block_of(k):
    n_col, n_chan = lax.axis_size("col"), lax.axis_size("chan")
    col = lax.rem(lax.axis_index("col") + k // n_chan, n_col)
    return col * n_chan + lax.rem(lax.axis_index("chan") + k % n_chan, n_chan)


def order_kernel(env_ref, order_ref, left_ref, turned_ref):
    env = env_ref[...].reshape(order_ref.shape[0], env_ref.shape[2])
    left_ref[...] = dot(order_ref[...], env).astype(BF16)
    turned_ref[...] = dot(env, order_ref[...], (((0,), (1,)), ((), ()))).astype(BF16)


def ordered(env, tile):
    channels, bonds, depth = env.shape
    size = tile * channels
    index = jnp.arange(size)
    wanted = (index % channels) * tile + index // channels
    order = (wanted[:, None] == index[None, :]).astype(BF16)
    return pl.pallas_call(
        order_kernel,
        grid=(bonds // tile,),
        in_specs=[
            pl.BlockSpec((channels, tile, depth), lambda i: (0, i, 0)),
            pl.BlockSpec((size, size), lambda i: (0, 0)),
        ],
        out_specs=[
            pl.BlockSpec((size, depth), lambda i: (i, 0)),
            pl.BlockSpec((depth, size), lambda i: (0, i)),
        ],
        out_shape=[
            jax.ShapeDtypeStruct((bonds * channels, depth), BF16),
            jax.ShapeDtypeStruct((depth, bonds * channels), BF16),
        ],
        compiler_params=params(),
        cost_estimate=cost(4 * size * env.size, 6 * env.size),
    )(env, order)


def part_kernel(scattered, env_ref, *outs):
    far, lanes = outs[0].shape
    count = lax.axis_size("col") * lax.axis_size("chan") if scattered else 1
    height = far // count
    for k in range(count):
        place = block_of(k) if scattered else k
        rows = pl.ds(pl.multiple_of(place * height, height), height)
        for h, out in enumerate(outs):
            out[k * height : (k + 1) * height] = env_ref[0, rows, h * lanes : (h + 1) * lanes]


def parted(env, lanes, scattered):
    channels, far, width = env.shape
    count = width // lanes
    return pl.pallas_call(
        functools.partial(part_kernel, scattered),
        grid=(channels,),
        in_specs=[pl.BlockSpec((1, far, width), lambda v: (v, 0, 0))],
        out_specs=[pl.BlockSpec((far, lanes), lambda v: (0, v))] * count,
        out_shape=[jax.ShapeDtypeStruct((far, channels * lanes), BF16)] * count,
        compiler_params=params(),
        cost_estimate=cost(0, 4 * env.size),
    )(env)


def fore_kernel(channels, lanes, n_outs, theta_ref, left_ref, mpo_ref, right_ref, *refs):
    outs, ones, threes = refs[-2 - n_outs : -2], refs[-2], refs[-1]
    phys_pair = theta_ref.shape[1] // lanes
    pair, step = 2 * channels, 2 * phys_pair
    pairs = left_ref.shape[0] // pair
    full = dot(left_ref[...], theta_ref[...])
    for i in range(pairs):
        for s in range(0, phys_pair, 2):
            both = [
                full[i * pair : (i + 1) * pair, q * lanes : (q + 1) * lanes] for q in (s, s + 1)
            ]
            ones[s * pair : (s + 2) * pair, i * lanes : (i + 1) * lanes] = jnp.concatenate(
                both, axis=0
            ).astype(BF16)
    mixed = dot(mpo_ref[...], ones[...]).astype(BF16)
    for i in range(pairs):
        for v in range(channels):
            threes[i * step : (i + 1) * step, v * lanes : (v + 1) * lanes] = mixed[
                v * step : (v + 1) * step, i * lanes : (i + 1) * lanes
            ]
    part = dot(right_ref[...], threes[...], ROWS)
    if len(refs) > 2 + n_outs:
        part = part + refs[0][...]
    height = outs[0].shape[0]
    for k, out in enumerate(outs):
        out[...] = part[k * height : (k + 1) * height].astype(out.dtype)


def fore(theta, left, mpo, right, total, channels, group, groups, kind, tile, place=0, n_outs=1):
    far = right.shape[0]
    lanes = right.shape[1] // channels
    phys_pair = theta.shape[1] // lanes
    bonds = left.shape[0] // channels // groups
    steps = bonds // tile
    totals = [] if total is None else [total]
    return pl.pallas_call(
        functools.partial(fore_kernel, channels, lanes, n_outs),
        grid=(steps,),
        in_specs=[
            pl.BlockSpec(theta.shape, lambda i: (0, 0), pipeline_mode=ONCE),
            pl.BlockSpec((tile * channels, left.shape[1]), lambda i: (group * steps + i, 0)),
            pl.BlockSpec(mpo.shape, lambda i: (0, 0), pipeline_mode=ONCE),
            pl.BlockSpec(right.shape, lambda i: (0, 0), pipeline_mode=ONCE),
        ]
        + [pl.BlockSpec((far, tile * phys_pair), lambda i: (0, place * steps + i))] * len(totals),
        out_specs=[pl.BlockSpec((far // n_outs, tile * phys_pair), lambda i: (0, i))] * n_outs,
        out_shape=[jax.ShapeDtypeStruct((far // n_outs, bonds * phys_pair), kind)] * n_outs,
        scratch_shapes=[
            pltpu.VMEM((2 * channels * phys_pair, tile // 2 * lanes), BF16),
            pltpu.VMEM((tile * phys_pair, channels * lanes), BF16),
        ],
        compiler_params=params(48),
        cost_estimate=cost(
            2 * bonds * phys_pair * right.shape[1] * (left.shape[1] + far)
            + bonds * mpo.size * lanes,
            2 * (theta.size + right.size + bonds * channels * left.shape[1])
            + 4 * far * bonds * phys_pair,
        ),
    )(theta, left, mpo, right, *totals)


def back_kernel(channels, n_parts, n_halves, *refs):
    parts = refs[:n_parts]
    mpo_ref, rights = refs[n_parts], refs[n_parts + 1 : n_parts + 1 + n_halves]
    outs, joined, ones = refs[-2 - n_halves : -2], refs[-2], refs[-1]
    lanes = rights[0].shape[1] // channels
    phys_pair = outs[0].shape[1] // lanes
    pair, step = 2 * channels, 2 * phys_pair
    pairs = outs[0].shape[0] // pair
    height = parts[0].shape[0]
    for k, part in enumerate(parts):
        joined[k * height : (k + 1) * height] = part[...]
    for right_ref, out_ref in zip(rights, outs):
        full = dot(joined[...], right_ref[...], COLS).astype(BF16)
        for i in range(pairs):
            for v in range(channels):
                ones[v * step : (v + 1) * step, i * lanes : (i + 1) * lanes] = full[
                    i * step : (i + 1) * step, v * lanes : (v + 1) * lanes
                ]
        mixed = dot(mpo_ref[...], ones[...])
        for i in range(0, pairs, 2):
            for s in range(phys_pair):
                both = [
                    mixed[s * pair : (s + 1) * pair, j * lanes : (j + 1) * lanes]
                    for j in (i, i + 1)
                ]
                out_ref[i * pair : (i + 2) * pair, s * lanes : (s + 1) * lanes] = jnp.concatenate(
                    both, axis=0
                ).astype(BF16)


def back(parts, mpo, rights, buffers, channels, phys_pair, group, groups, tile):
    columns = parts[0].shape[1]
    bonds = columns // phys_pair
    far, width = rights[0].shape
    lanes = width // channels
    steps = bonds // tile
    count = len(rights)
    before = len(parts) + 1 + count
    return pl.pallas_call(
        functools.partial(back_kernel, channels, len(parts), count),
        grid=(steps,),
        input_output_aliases={before + k: k for k in range(len(buffers))},
        in_specs=[pl.BlockSpec((p.shape[0], tile * phys_pair), lambda i: (0, i)) for p in parts]
        + [pl.BlockSpec(mpo.shape, lambda i: (0, 0), pipeline_mode=ONCE)]
        + [pl.BlockSpec((far, width), lambda i: (0, 0), pipeline_mode=ONCE)] * count
        + [ANY] * len(buffers),
        out_specs=[
            pl.BlockSpec((tile * channels, phys_pair * lanes), lambda i: (group * steps + i, 0))
        ]
        * count,
        out_shape=[jax.ShapeDtypeStruct((groups * bonds * channels, phys_pair * lanes), BF16)]
        * count,
        scratch_shapes=[
            pltpu.VMEM((far, tile * phys_pair), BF16),
            pltpu.VMEM((2 * channels * phys_pair, tile // 2 * lanes), BF16),
        ],
        compiler_params=params(48),
        cost_estimate=cost(
            count * (2 * far * width * columns + bonds * mpo.size * lanes),
            2 * count * (far * width + bonds * channels * phys_pair * lanes) + 2 * far * columns,
        ),
    )(*parts, mpo, *rights, *buffers)


def last_kernel(left_ref, back_ref, out_ref):
    out_ref[...] = dot(left_ref[...], back_ref[...]).astype(BF16)


def last(left_t, backs, chunk, n_chunks):
    columns = backs.shape[1] // n_chunks
    steps = 2
    return pl.pallas_call(
        last_kernel,
        grid=(steps,),
        in_specs=[
            pl.BlockSpec(left_t.shape, lambda i: (0, 0), pipeline_mode=ONCE),
            pl.BlockSpec((backs.shape[0], columns // steps), lambda i: (0, chunk * steps + i)),
        ],
        out_specs=pl.BlockSpec((left_t.shape[0], columns // steps), lambda i: (0, i)),
        out_shape=jax.ShapeDtypeStruct((left_t.shape[0], columns), BF16),
        compiler_params=params(48),
        cost_estimate=cost(
            2 * left_t.size * columns,
            2 * (left_t.size + left_t.shape[1] * columns + left_t.shape[0] * columns),
        ),
    )(left_t, backs)


def join_kernel(n_rows, n_parts, *refs):
    blocks, out, sems = refs[:-2], refs[-2], refs[-1]
    depth, columns = blocks[0].shape
    reach = 2 * n_rows - 1
    for phase in ("start", "wait"):
        for k, block in enumerate(blocks):
            source = lax.axis_index("row") + (k % reach - (n_rows - 1))

            @pl.when((source >= 0) & (source < n_rows))
            def _():
                target = out.at[
                    pl.ds(pl.multiple_of(source * depth, depth), depth),
                    pl.ds(k // reach * columns, columns),
                ]
                getattr(pltpu.make_async_copy(block, target, sems.at[k]), phase)()


def join(parts, n_rows):
    blocks = [block for part in parts for block in part]
    depth, columns = blocks[0].shape
    return pl.pallas_call(
        functools.partial(join_kernel, n_rows, len(parts)),
        in_specs=[ANY] * len(blocks),
        out_specs=pl.BlockSpec(memory_space=pltpu.VMEM),
        out_shape=jax.ShapeDtypeStruct((depth * n_rows, columns * len(parts)), BF16),
        scratch_shapes=[pltpu.SemaphoreType.DMA((len(blocks),))],
        compiler_params=params(),
        cost_estimate=cost(0, 4 * depth * n_rows * columns * len(parts)),
    )(*blocks)


def after(arrays, *deps):
    return lax.optimization_barrier((arrays, deps))[0]


def gather_round(pair, t, n_rows):
    up = lax.ppermute(pair[0], "row", [(r, r + 1) for r in range(t - 1, n_rows - 1)])
    down = lax.ppermute(pair[1], "row", [(r, r - 1) for r in range(1, n_rows - t + 1)])
    return up, down


def row_block(term, distance, n_rows):
    height = term.shape[0] // n_rows
    block = lax.rem(lax.axis_index("row") + distance, n_rows)
    return lax.dynamic_slice_in_dim(term, block * height, height)


def scatter_inputs(term, pair, t, n_rows):
    up, down = row_block(term, n_rows - t, n_rows), row_block(term, t, n_rows)
    if pair is not None:
        up, down = add(up, pair[0]), add(down, pair[1])
    return lax.optimization_barrier((up, down))


def scatter_round(pair, t, n_rows):
    up = lax.ppermute(pair[0], "row", [(r, r + 1) for r in range(t)])
    down = lax.ppermute(pair[1], "row", [(n_rows - 1 - r, n_rows - 2 - r) for r in range(t)])
    return up, down


def add(x, y):
    return (x.astype(F32) + y.astype(F32)).astype(BF16)


def swapped(block, axis):
    return lax.ppermute(block, axis, [(0, 1), (1, 0)])


def shards(theta, left_env, right_env, mpo_left, mpo_right):
    bonds, channels, depth = left_env.shape
    rows, phys_pair, width = theta.shape
    n_rows = lax.axis_size("row")
    scattered = lax.axis_size("col") == 2 and lax.axis_size("chan") == 2
    tile = min(32, bonds)
    lanes = min(128, width)
    halves = width // lanes
    groups = max(1, min(4, bonds // tile))
    n_chunks = 2
    per = phys_pair // n_chunks

    def mpo_pairs(*deps):
        one, two = after((mpo_left, mpo_right), *deps)
        paired = jnp.einsum("wuxs,uvyt->wstxyv", one, two, precision=lax.Precision.HIGHEST)
        mpo = paired.reshape(channels, phys_pair, phys_pair, channels).astype(BF16)
        twice = jnp.einsum("wsxv,jk->sjwvkx", mpo, jnp.eye(2, dtype=BF16))
        size = 2 * channels * phys_pair
        mpo_back = twice.reshape(size, size)
        return mpo_back.T, mpo_back

    def far_parts(*deps):
        return parted(after(right_env, *deps).transpose(1, 0, 2), lanes, scattered)

    left, left_t = ordered(left_env.transpose(1, 0, 2), tile)
    if halves == 1 or n_rows == 2:
        mpo_fore, mpo_back = mpo_pairs()
    right = far_parts() if halves == 1 else None

    theta_all, total, last_round = None, [None], [()] * n_chunks
    cuts = 2 if groups % 2 == 0 and n_rows > 2 else 1
    for h in range(halves):
        cut = theta[:, :, h * lanes : (h + 1) * lanes]
        pairs, blocks, fresh = [], [], []

        def ahead(*deps):
            return fore(
                after(theta_all, *deps, *fresh), left, mpo_fore, right[h - 1], total[0], channels,
                len(fresh), cuts, F32, tile,
            )

        for c in range(n_chunks):
            piece = cut[:, c * per : (c + 1) * per].reshape(rows, per * lanes)
            pairs.append(after((piece, piece), *last_round[c]))
            blocks.append([piece])
        for t in range(1, n_rows):
            came = list(pairs)
            if (h, t) == (0, 2):
                pairs[0] = after(pairs[0], left, left_t)
                if halves > 1:
                    mpo_fore, mpo_back = mpo_pairs(*pairs)
            if (h, t) == (0, 3) and halves > 1:
                pairs[0] = after(pairs[0], mpo_fore, mpo_back)
            if (h, t) == (1, 2):
                pairs = [after(pair, right, theta_all) for pair in pairs]
            if h > 0 and t > 2 and len(fresh) < cuts:
                fresh += ahead(*sent)
                pairs = [after(pair, fresh[-1]) for pair in pairs]
            sent = came
            for c in range(n_chunks):
                pairs[c] = gather_round(pairs[c], t, n_rows)
                blocks[c] = [pairs[c][0]] + blocks[c] + [pairs[c][1]]
        while h > 0 and len(fresh) < cuts:
            fresh += ahead(*sent)
        total = fresh or total
        last_round = pairs
        if h == 0 and halves > 1:
            right = far_parts(*pairs)
        theta_all = join(after(blocks, *fresh), n_rows)

    def forward(g, *deps):
        here = g * len(total) // groups
        return fore(
            after(theta_all, *deps), left, mpo_fore, right[-1], total[here], channels, g, groups,
            BF16, tile, g % (groups // len(total)), 2 if scattered else 1,
        )

    def backward(g, backs, *deps):
        parts = after(everyone[g], *deps)
        return back(parts, mpo_back, right, backs, channels, phys_pair, g, groups, tile)

    terms, near, own, far, everyone, backs = [], [], [], [], [], []
    step = 0
    while len(everyone) < groups or step < 2 * groups:
        g = step - groups
        waits = []
        if scattered:
            for lag, done in ((2, near), (3, own), (4, far)):
                waits += done[step - lag : step - lag + 1] if step >= lag else []
        if step < groups:
            terms.append(forward(step, *waits))
            out = terms[-1][0]
        elif 0 <= g < len(everyone):
            backs = backward(g, backs, *waits)
            out = backs[-1]
        step += 1
        if not scattered:
            if step <= groups:
                own.append(lax.psum_scatter(out, ("col", "chan"), scatter_dimension=0, tiled=True))
                everyone.append([lax.all_gather(own[-1], ("col", "chan"), axis=0, tiled=True)])
            continue
        if len(everyone) < len(far):
            across = after(far[len(everyone)], out)
            pair = [own[len(everyone)], across]
            everyone.append(pair + [swapped(x, "col") for x in pair])
        if len(far) < len(own):
            far.append(swapped(after(own[len(far)], out), "chan"))
        if len(own) < len(near):
            both = after(near[len(own)], out)
            height = both.shape[0] // 2
            own.append(add(both[:height], swapped(both[height:], "chan")))
        if len(near) < len(terms):
            mine, other = terms[len(near)]
            near.append(add(mine, swapped(other, "col")))
    for g in range(step - groups, groups):
        backs = backward(g, backs)

    terms, rounds = [], []

    def advance(i, *deps):
        t = len(rounds[i]) + 1
        if t < n_rows:
            pair = after(rounds[i][-1], *deps) if t > 1 else None
            ready = scatter_inputs(terms[i], pair, t, n_rows)
            rounds[i].append(scatter_round(ready, t, n_rows))
            return list(ready)

    def come(i, t):
        return list(rounds[i][min(t, len(rounds[i])) - 1])

    for i in range(halves * n_chunks):
        waits = sent + terms[-1:] if i > 0 else []
        waits += come(i - 2, 1) if i > 1 else []
        waits += come(i - 3, 2) if i > 2 else []
        terms.append(last(left_t, after(backs[i // n_chunks], *waits), i % n_chunks, n_chunks))
        rounds.append([])
        for j in range(i + 1):
            sent = advance(j, terms[-1])
    products = []
    for i in range(len(terms)):
        while len(rounds[i]) < n_rows - 1:
            advance(i)
        total = row_block(terms[i], 0, n_rows).astype(F32)
        for x in rounds[i][-1]:
            total = total + x.astype(F32)
        products.append(total.astype(BF16).reshape(rows, per, lanes))
    products = [
        jnp.concatenate(products[h * n_chunks : (h + 1) * n_chunks], axis=1) for h in range(halves)
    ]
    return jnp.concatenate(own, axis=1), jnp.concatenate(products, axis=2)


def solution(mesh):
    in_specs = (
        P(("grp", "row"), None, ("col", "chan")),
        P(("grp", "row"), None, None),
        P("grp", None, ("col", "chan")),
        P(),
        P(),
    )
    out_specs = (P(("grp", "col", "chan"), "row"), P(("grp", "row"), None, ("col", "chan")))
    return jax.shard_map(shards, mesh=mesh, in_specs=in_specs, out_specs=out_specs, check_vma=False)
```

```python
import functools

import jax
import jax.numpy as jnp
from jax import lax
from jax.experimental import pallas as pl
from jax.experimental.pallas import tpu as pltpu
from jax.sharding import PartitionSpec as P

BF16 = jnp.bfloat16
F32 = jnp.float32
MIB = 1024 * 1024
LINES = (((1,), (0,)), ((), ()))
ROWS = (((1,), (1,)), ((), ()))
COLS = (((0,), (0,)), ((), ()))
ANY = pl.BlockSpec(memory_space=pl.ANY)
ONCE = pl.Buffered(1)


def dot(x, y, dims=LINES):
    return lax.dot_general(x, y, dims, preferred_element_type=F32)


def params(limit=56):
    return pltpu.CompilerParams(vmem_limit_bytes=limit * MIB)


def cost(flops, moved):
    return pl.CostEstimate(flops=int(flops), bytes_accessed=int(moved), transcendentals=0)


def block_of(k):
    n_col, n_chan = lax.axis_size("col"), lax.axis_size("chan")
    col = lax.rem(lax.axis_index("col") + k // n_chan, n_col)
    return col * n_chan + lax.rem(lax.axis_index("chan") + k % n_chan, n_chan)


def order_kernel(env_ref, order_ref, left_ref, turned_ref):
    env = env_ref[...].reshape(order_ref.shape[0], env_ref.shape[2])
    left_ref[...] = dot(order_ref[...], env).astype(BF16)
    turned_ref[...] = dot(env, order_ref[...], (((0,), (1,)), ((), ()))).astype(BF16)


def ordered(env, tile):
    channels, bonds, depth = env.shape
    size = tile * channels
    index = jnp.arange(size)
    wanted = (index % channels) * tile + index // channels
    order = (wanted[:, None] == index[None, :]).astype(BF16)
    return pl.pallas_call(
        order_kernel,
        grid=(bonds // tile,),
        in_specs=[
            pl.BlockSpec((channels, tile, depth), lambda i: (0, i, 0)),
            pl.BlockSpec((size, size), lambda i: (0, 0)),
        ],
        out_specs=[
            pl.BlockSpec((size, depth), lambda i: (i, 0)),
            pl.BlockSpec((depth, size), lambda i: (0, i)),
        ],
        out_shape=[
            jax.ShapeDtypeStruct((bonds * channels, depth), BF16),
            jax.ShapeDtypeStruct((depth, bonds * channels), BF16),
        ],
        compiler_params=params(),
        cost_estimate=cost(4 * size * env.size, 6 * env.size),
    )(env, order)


def part_kernel(scattered, env_ref, *outs):
    far, lanes = outs[0].shape
    count = lax.axis_size("col") * lax.axis_size("chan") if scattered else 1
    height = far // count
    for k in range(count):
        place = block_of(k) if scattered else k
        rows = pl.ds(pl.multiple_of(place * height, height), height)
        for h, out in enumerate(outs):
            out[k * height : (k + 1) * height] = env_ref[0, rows, h * lanes : (h + 1) * lanes]


def parted(env, lanes, scattered):
    channels, far, width = env.shape
    count = width // lanes
    return pl.pallas_call(
        functools.partial(part_kernel, scattered),
        grid=(channels,),
        in_specs=[pl.BlockSpec((1, far, width), lambda v: (v, 0, 0))],
        out_specs=[pl.BlockSpec((far, lanes), lambda v: (0, v))] * count,
        out_shape=[jax.ShapeDtypeStruct((far, channels * lanes), BF16)] * count,
        compiler_params=params(),
        cost_estimate=cost(0, 4 * env.size),
    )(env)


def fore_kernel(channels, lanes, n_outs, theta_ref, left_ref, mpo_ref, right_ref, *refs):
    outs, ones, threes = refs[-2 - n_outs : -2], refs[-2], refs[-1]
    phys_pair = theta_ref.shape[1] // lanes
    pair, step = 2 * channels, 2 * phys_pair
    pairs = left_ref.shape[0] // pair
    full = dot(left_ref[...], theta_ref[...])
    for i in range(pairs):
        for s in range(0, phys_pair, 2):
            both = [
                full[i * pair : (i + 1) * pair, q * lanes : (q + 1) * lanes] for q in (s, s + 1)
            ]
            ones[s * pair : (s + 2) * pair, i * lanes : (i + 1) * lanes] = jnp.concatenate(
                both, axis=0
            ).astype(BF16)
    mixed = dot(mpo_ref[...], ones[...]).astype(BF16)
    for i in range(pairs):
        for v in range(channels):
            threes[i * step : (i + 1) * step, v * lanes : (v + 1) * lanes] = mixed[
                v * step : (v + 1) * step, i * lanes : (i + 1) * lanes
            ]
    part = dot(right_ref[...], threes[...], ROWS)
    if len(refs) > 2 + n_outs:
        part = part + refs[0][...]
    height = outs[0].shape[0]
    for k, out in enumerate(outs):
        out[...] = part[k * height : (k + 1) * height].astype(out.dtype)


def fore(theta, left, mpo, right, total, channels, group, groups, kind, tile, place=0, n_outs=1):
    far = right.shape[0]
    lanes = right.shape[1] // channels
    phys_pair = theta.shape[1] // lanes
    bonds = left.shape[0] // channels // groups
    steps = bonds // tile
    totals = [] if total is None else [total]
    return pl.pallas_call(
        functools.partial(fore_kernel, channels, lanes, n_outs),
        grid=(steps,),
        in_specs=[
            pl.BlockSpec(theta.shape, lambda i: (0, 0), pipeline_mode=ONCE),
            pl.BlockSpec((tile * channels, left.shape[1]), lambda i: (group * steps + i, 0)),
            pl.BlockSpec(mpo.shape, lambda i: (0, 0), pipeline_mode=ONCE),
            pl.BlockSpec(right.shape, lambda i: (0, 0), pipeline_mode=ONCE),
        ]
        + [pl.BlockSpec((far, tile * phys_pair), lambda i: (0, place * steps + i))] * len(totals),
        out_specs=[pl.BlockSpec((far // n_outs, tile * phys_pair), lambda i: (0, i))] * n_outs,
        out_shape=[jax.ShapeDtypeStruct((far // n_outs, bonds * phys_pair), kind)] * n_outs,
        scratch_shapes=[
            pltpu.VMEM((2 * channels * phys_pair, tile // 2 * lanes), BF16),
            pltpu.VMEM((tile * phys_pair, channels * lanes), BF16),
        ],
        compiler_params=params(48),
        cost_estimate=cost(
            2 * bonds * phys_pair * right.shape[1] * (left.shape[1] + far)
            + bonds * mpo.size * lanes,
            2 * (theta.size + right.size + bonds * channels * left.shape[1])
            + 4 * far * bonds * phys_pair,
        ),
    )(theta, left, mpo, right, *totals)


def back_kernel(channels, n_parts, n_halves, *refs):
    parts = refs[:n_parts]
    mpo_ref, rights = refs[n_parts], refs[n_parts + 1 : n_parts + 1 + n_halves]
    outs, joined, ones = refs[-2 - n_halves : -2], refs[-2], refs[-1]
    lanes = rights[0].shape[1] // channels
    phys_pair = outs[0].shape[1] // lanes
    pair, step = 2 * channels, 2 * phys_pair
    pairs = outs[0].shape[0] // pair
    height = parts[0].shape[0]
    for k, part in enumerate(parts):
        joined[k * height : (k + 1) * height] = part[...]
    for right_ref, out_ref in zip(rights, outs):
        full = dot(joined[...], right_ref[...], COLS).astype(BF16)
        for i in range(pairs):
            for v in range(channels):
                ones[v * step : (v + 1) * step, i * lanes : (i + 1) * lanes] = full[
                    i * step : (i + 1) * step, v * lanes : (v + 1) * lanes
                ]
        mixed = dot(mpo_ref[...], ones[...])
        for i in range(0, pairs, 2):
            for s in range(phys_pair):
                both = [
                    mixed[s * pair : (s + 1) * pair, j * lanes : (j + 1) * lanes]
                    for j in (i, i + 1)
                ]
                out_ref[i * pair : (i + 2) * pair, s * lanes : (s + 1) * lanes] = jnp.concatenate(
                    both, axis=0
                ).astype(BF16)


def back(parts, mpo, rights, buffers, channels, phys_pair, group, groups, tile):
    columns = parts[0].shape[1]
    bonds = columns // phys_pair
    far, width = rights[0].shape
    lanes = width // channels
    steps = bonds // tile
    count = len(rights)
    before = len(parts) + 1 + count
    return pl.pallas_call(
        functools.partial(back_kernel, channels, len(parts), count),
        grid=(steps,),
        input_output_aliases={before + k: k for k in range(len(buffers))},
        in_specs=[pl.BlockSpec((p.shape[0], tile * phys_pair), lambda i: (0, i)) for p in parts]
        + [pl.BlockSpec(mpo.shape, lambda i: (0, 0), pipeline_mode=ONCE)]
        + [pl.BlockSpec((far, width), lambda i: (0, 0), pipeline_mode=ONCE)] * count
        + [ANY] * len(buffers),
        out_specs=[
            pl.BlockSpec((tile * channels, phys_pair * lanes), lambda i: (group * steps + i, 0))
        ]
        * count,
        out_shape=[jax.ShapeDtypeStruct((groups * bonds * channels, phys_pair * lanes), BF16)]
        * count,
        scratch_shapes=[
            pltpu.VMEM((far, tile * phys_pair), BF16),
            pltpu.VMEM((2 * channels * phys_pair, tile // 2 * lanes), BF16),
        ],
        compiler_params=params(48),
        cost_estimate=cost(
            count * (2 * far * width * columns + bonds * mpo.size * lanes),
            2 * count * (far * width + bonds * channels * phys_pair * lanes) + 2 * far * columns,
        ),
    )(*parts, mpo, *rights, *buffers)


def last_kernel(left_ref, back_ref, out_ref):
    out_ref[...] = dot(left_ref[...], back_ref[...]).astype(BF16)


def last(left_t, backs, chunk, n_chunks):
    columns = backs.shape[1] // n_chunks
    steps = 2
    return pl.pallas_call(
        last_kernel,
        grid=(steps,),
        in_specs=[
            pl.BlockSpec(left_t.shape, lambda i: (0, 0), pipeline_mode=ONCE),
            pl.BlockSpec((backs.shape[0], columns // steps), lambda i: (0, chunk * steps + i)),
        ],
        out_specs=pl.BlockSpec((left_t.shape[0], columns // steps), lambda i: (0, i)),
        out_shape=jax.ShapeDtypeStruct((left_t.shape[0], columns), BF16),
        compiler_params=params(48),
        cost_estimate=cost(
            2 * left_t.size * columns,
            2 * (left_t.size + left_t.shape[1] * columns + left_t.shape[0] * columns),
        ),
    )(left_t, backs)


def join_kernel(n_rows, n_parts, *refs):
    blocks, out, sems = refs[:-2], refs[-2], refs[-1]
    depth, columns = blocks[0].shape
    reach = 2 * n_rows - 1
    for phase in ("start", "wait"):
        for k, block in enumerate(blocks):
            source = lax.axis_index("row") + (k % reach - (n_rows - 1))

            @pl.when((source >= 0) & (source < n_rows))
            def _():
                target = out.at[
                    pl.ds(pl.multiple_of(source * depth, depth), depth),
                    pl.ds(k // reach * columns, columns),
                ]
                getattr(pltpu.make_async_copy(block, target, sems.at[k]), phase)()


def join(parts, n_rows):
    blocks = [block for part in parts for block in part]
    depth, columns = blocks[0].shape
    return pl.pallas_call(
        functools.partial(join_kernel, n_rows, len(parts)),
        in_specs=[ANY] * len(blocks),
        out_specs=pl.BlockSpec(memory_space=pltpu.VMEM),
        out_shape=jax.ShapeDtypeStruct((depth * n_rows, columns * len(parts)), BF16),
        scratch_shapes=[pltpu.SemaphoreType.DMA((len(blocks),))],
        compiler_params=params(),
        cost_estimate=cost(0, 4 * depth * n_rows * columns * len(parts)),
    )(*blocks)


def after(arrays, *deps):
    return lax.optimization_barrier((arrays, deps))[0]


def gather_round(pair, t, n_rows):
    up = lax.ppermute(pair[0], "row", [(r, r + 1) for r in range(t - 1, n_rows - 1)])
    down = lax.ppermute(pair[1], "row", [(r, r - 1) for r in range(1, n_rows - t + 1)])
    return up, down


def row_block(term, distance, n_rows):
    height = term.shape[0] // n_rows
    block = lax.rem(lax.axis_index("row") + distance, n_rows)
    return lax.dynamic_slice_in_dim(term, block * height, height)


def scatter_inputs(term, pair, t, n_rows):
    up, down = row_block(term, n_rows - t, n_rows), row_block(term, t, n_rows)
    if pair is not None:
        up, down = add(up, pair[0]), add(down, pair[1])
    return lax.optimization_barrier((up, down))


def scatter_round(pair, t, n_rows):
    up = lax.ppermute(pair[0], "row", [(r, r + 1) for r in range(t)])
    down = lax.ppermute(pair[1], "row", [(n_rows - 1 - r, n_rows - 2 - r) for r in range(t)])
    return up, down


def add(x, y):
    return (x.astype(F32) + y.astype(F32)).astype(BF16)


def swapped(block, axis):
    return lax.ppermute(block, axis, [(0, 1), (1, 0)])


def scattered_along(both):
    height = both.shape[0] // 2
    return add(both[:height], swapped(both[height:], "chan"))


def shards(theta, left_env, right_env, mpo_left, mpo_right):
    bonds, channels, depth = left_env.shape
    rows, phys_pair, width = theta.shape
    n_rows = lax.axis_size("row")
    scattered = lax.axis_size("col") == 2 and lax.axis_size("chan") == 2
    tile = min(32, bonds)
    lanes = min(128, width)
    halves = width // lanes
    groups = max(1, min(4, bonds // tile))
    n_chunks = 2
    per = phys_pair // n_chunks

    def mpo_pairs(*deps):
        one, two = after((mpo_left, mpo_right), *deps)
        paired = jnp.einsum("wuxs,uvyt->wstxyv", one, two, precision=lax.Precision.HIGHEST)
        mpo = paired.reshape(channels, phys_pair, phys_pair, channels).astype(BF16)
        twice = jnp.einsum("wsxv,jk->sjwvkx", mpo, jnp.eye(2, dtype=BF16))
        size = 2 * channels * phys_pair
        mpo_back = twice.reshape(size, size)
        return mpo_back.T, mpo_back

    def far_parts(*deps):
        return parted(after(right_env, *deps).transpose(1, 0, 2), lanes, scattered)

    left, left_t = ordered(left_env.transpose(1, 0, 2), tile)
    if halves == 1 or n_rows == 2:
        mpo_fore, mpo_back = mpo_pairs()
    right = far_parts() if halves == 1 else None

    theta_all, total, last_round = None, [None], [()] * n_chunks
    cuts = 2 if groups % 2 == 0 and n_rows > 2 else 1
    for h in range(halves):
        cut = theta[:, :, h * lanes : (h + 1) * lanes]
        pairs, blocks, fresh = [], [], []

        def ahead(*deps):
            return fore(
                after(theta_all, *deps, *fresh), left, mpo_fore, right[h - 1], total[0], channels,
                len(fresh), cuts, F32, tile,
            )

        for c in range(n_chunks):
            piece = cut[:, c * per : (c + 1) * per].reshape(rows, per * lanes)
            pairs.append(after((piece, piece), *last_round[c]))
            blocks.append([piece])
        for t in range(1, n_rows):
            came = list(pairs)
            if (h, t) == (0, 2):
                pairs[0] = after(pairs[0], left, left_t)
                if halves > 1:
                    mpo_fore, mpo_back = mpo_pairs(*pairs)
            if (h, t) == (0, 3) and halves > 1:
                pairs[0] = after(pairs[0], mpo_fore, mpo_back)
            if (h, t) == (1, 2):
                pairs = [after(pair, right, theta_all) for pair in pairs]
            if h > 0 and t > 2 and len(fresh) < cuts:
                fresh += ahead(*sent)
                pairs = [after(pair, fresh[-1]) for pair in pairs]
            sent = came
            for c in range(n_chunks):
                pairs[c] = gather_round(pairs[c], t, n_rows)
                blocks[c] = [pairs[c][0]] + blocks[c] + [pairs[c][1]]
        while h > 0 and len(fresh) < cuts:
            fresh += ahead(*sent)
        total = fresh or total
        last_round = pairs
        if h == 0 and halves > 1:
            right = far_parts(*pairs)
        theta_all = join(after(blocks, *fresh), n_rows)

    def forward(g, *deps):
        here = g * len(total) // groups
        return fore(
            after(theta_all, *deps), left, mpo_fore, right[-1], total[here], channels, g, groups,
            BF16, tile, g % (groups // len(total)), 2 if scattered else 1,
        )

    def backward(g, backs, *deps):
        parts = after(everyone[g], *deps)
        return back(parts, mpo_back, right, backs, channels, phys_pair, g, groups, tile)

    terms, near, own, far, everyone, backs = [], [], [], [], [], []
    step = 0
    while len(everyone) < groups or step < 2 * groups:
        g = step - groups
        waits = []
        if scattered:
            for lag, done in ((2, near), (3, own), (4, far)):
                waits += done[step - lag : step - lag + 1] if step >= lag else []
                waits += done[:1] if step == lag - 1 else []
        if step < groups:
            terms.append(forward(step, *waits))
            out = terms[-1][0]
        elif 0 <= g < len(everyone):
            backs = backward(g, backs, *waits)
            out = backs[-1]
        step += 1
        if not scattered:
            if step <= groups:
                own.append(lax.psum_scatter(out, ("col", "chan"), scatter_dimension=0, tiled=True))
                everyone.append([lax.all_gather(own[-1], ("col", "chan"), axis=0, tiled=True)])
            continue
        if len(everyone) < len(far):
            across = after(far[len(everyone)], out)
            pair = [own[len(everyone)], across]
            everyone.append(pair + [swapped(x, "col") for x in pair])
        if len(far) < len(own):
            far.append(swapped(after(own[len(far)], out), "chan"))
        if len(own) < len(near):
            own.append(scattered_along(after(near[len(own)], out)))
        if len(near) < len(terms):
            mine, other = terms[len(near)]
            near.append(add(mine, swapped(other, "col")))
        if step == 1:
            own.append(scattered_along(near[0]))
    for g in range(step - groups, groups):
        backs = backward(g, backs)

    terms, rounds = [], []

    def advance(i, *deps):
        t = len(rounds[i]) + 1
        if t < n_rows:
            pair = after(rounds[i][-1], *deps) if t > 1 else None
            ready = scatter_inputs(terms[i], pair, t, n_rows)
            rounds[i].append(scatter_round(ready, t, n_rows))
            return list(ready)

    def come(i, t):
        return list(rounds[i][min(t, len(rounds[i])) - 1])

    for i in range(halves * n_chunks):
        waits = sent + terms[-1:] if i > 0 else []
        waits += come(i - 2, 1) if i > 1 else []
        waits += come(i - 3, 2) if i > 2 else []
        terms.append(last(left_t, after(backs[i // n_chunks], *waits), i % n_chunks, n_chunks))
        rounds.append([])
        for j in range(i + 1):
            sent = advance(j, terms[-1])
    products = []
    for i in range(len(terms)):
        while len(rounds[i]) < n_rows - 1:
            advance(i)
        total = row_block(terms[i], 0, n_rows).astype(F32)
        for x in rounds[i][-1]:
            total = total + x.astype(F32)
        products.append(total.astype(BF16).reshape(rows, per, lanes))
    products = [
        jnp.concatenate(products[h * n_chunks : (h + 1) * n_chunks], axis=1) for h in range(halves)
    ]
    return jnp.concatenate(own, axis=1), jnp.concatenate(products, axis=2)


def solution(mesh):
    in_specs = (
        P(("grp", "row"), None, ("col", "chan")),
        P(("grp", "row"), None, None),
        P("grp", None, ("col", "chan")),
        P(),
        P(),
    )
    out_specs = (P(("grp", "col", "chan"), "row"), P(("grp", "row"), None, ("col", "chan")))
    return jax.shard_map(shards, mesh=mesh, in_specs=in_specs, out_specs=out_specs, check_vma=False)
```

```python
import functools

import jax
import jax.numpy as jnp
from jax import lax
from jax.experimental import pallas as pl
from jax.experimental.pallas import tpu as pltpu
from jax.sharding import PartitionSpec as P

BF16 = jnp.bfloat16
F32 = jnp.float32
MIB = 1024 * 1024
LINES = (((1,), (0,)), ((), ()))
ROWS = (((1,), (1,)), ((), ()))
COLS = (((0,), (0,)), ((), ()))
ANY = pl.BlockSpec(memory_space=pl.ANY)
ONCE = pl.Buffered(1)


def dot(x, y, dims=LINES):
    return lax.dot_general(x, y, dims, preferred_element_type=F32)


def params(limit=56):
    return pltpu.CompilerParams(vmem_limit_bytes=limit * MIB)


def cost(flops, moved):
    return pl.CostEstimate(flops=int(flops), bytes_accessed=int(moved), transcendentals=0)


def block_of(k):
    n_col, n_chan = lax.axis_size("col"), lax.axis_size("chan")
    col = lax.rem(lax.axis_index("col") + k // n_chan, n_col)
    return col * n_chan + lax.rem(lax.axis_index("chan") + k % n_chan, n_chan)


def order_kernel(env_ref, order_ref, left_ref, turned_ref):
    env = env_ref[...].reshape(order_ref.shape[0], env_ref.shape[2])
    left_ref[...] = dot(order_ref[...], env).astype(BF16)
    turned_ref[...] = dot(env, order_ref[...], (((0,), (1,)), ((), ()))).astype(BF16)


def ordered(env, tile):
    channels, bonds, depth = env.shape
    size = tile * channels
    index = jnp.arange(size)
    wanted = (index % channels) * tile + index // channels
    order = (wanted[:, None] == index[None, :]).astype(BF16)
    return pl.pallas_call(
        order_kernel,
        grid=(bonds // tile,),
        in_specs=[
            pl.BlockSpec((channels, tile, depth), lambda i: (0, i, 0)),
            pl.BlockSpec((size, size), lambda i: (0, 0)),
        ],
        out_specs=[
            pl.BlockSpec((size, depth), lambda i: (i, 0)),
            pl.BlockSpec((depth, size), lambda i: (0, i)),
        ],
        out_shape=[
            jax.ShapeDtypeStruct((bonds * channels, depth), BF16),
            jax.ShapeDtypeStruct((depth, bonds * channels), BF16),
        ],
        compiler_params=params(),
        cost_estimate=cost(4 * size * env.size, 6 * env.size),
    )(env, order)


def part_kernel(scattered, env_ref, *outs):
    far, lanes = outs[0].shape
    count = lax.axis_size("col") * lax.axis_size("chan") if scattered else 1
    height = far // count
    for k in range(count):
        place = block_of(k) if scattered else k
        rows = pl.ds(pl.multiple_of(place * height, height), height)
        for h, out in enumerate(outs):
            out[k * height : (k + 1) * height] = env_ref[0, rows, h * lanes : (h + 1) * lanes]


def parted(env, lanes, scattered):
    channels, far, width = env.shape
    count = width // lanes
    return pl.pallas_call(
        functools.partial(part_kernel, scattered),
        grid=(channels,),
        in_specs=[pl.BlockSpec((1, far, width), lambda v: (v, 0, 0))],
        out_specs=[pl.BlockSpec((far, lanes), lambda v: (0, v))] * count,
        out_shape=[jax.ShapeDtypeStruct((far, channels * lanes), BF16)] * count,
        compiler_params=params(),
        cost_estimate=cost(0, 4 * env.size),
    )(env)


def fore_kernel(channels, lanes, n_outs, theta_ref, left_ref, mpo_ref, right_ref, *refs):
    outs, ones, threes = refs[-2 - n_outs : -2], refs[-2], refs[-1]
    phys_pair = theta_ref.shape[1] // lanes
    pair, step = 2 * channels, 2 * phys_pair
    pairs = left_ref.shape[0] // pair
    full = dot(left_ref[...], theta_ref[...])
    for i in range(pairs):
        for s in range(0, phys_pair, 2):
            both = [
                full[i * pair : (i + 1) * pair, q * lanes : (q + 1) * lanes] for q in (s, s + 1)
            ]
            ones[s * pair : (s + 2) * pair, i * lanes : (i + 1) * lanes] = jnp.concatenate(
                both, axis=0
            ).astype(BF16)
    mixed = dot(mpo_ref[...], ones[...]).astype(BF16)
    for i in range(pairs):
        for v in range(channels):
            threes[i * step : (i + 1) * step, v * lanes : (v + 1) * lanes] = mixed[
                v * step : (v + 1) * step, i * lanes : (i + 1) * lanes
            ]
    part = dot(right_ref[...], threes[...], ROWS)
    if len(refs) > 2 + n_outs:
        part = part + refs[0][...]
    height = outs[0].shape[0]
    for k, out in enumerate(outs):
        out[...] = part[k * height : (k + 1) * height].astype(out.dtype)


def fore(theta, left, mpo, right, total, channels, group, groups, kind, tile, place=0, n_outs=1):
    far = right.shape[0]
    lanes = right.shape[1] // channels
    phys_pair = theta.shape[1] // lanes
    bonds = left.shape[0] // channels // groups
    steps = bonds // tile
    totals = [] if total is None else [total]
    return pl.pallas_call(
        functools.partial(fore_kernel, channels, lanes, n_outs),
        grid=(steps,),
        in_specs=[
            pl.BlockSpec(theta.shape, lambda i: (0, 0), pipeline_mode=ONCE),
            pl.BlockSpec((tile * channels, left.shape[1]), lambda i: (group * steps + i, 0)),
            pl.BlockSpec(mpo.shape, lambda i: (0, 0), pipeline_mode=ONCE),
            pl.BlockSpec(right.shape, lambda i: (0, 0), pipeline_mode=ONCE),
        ]
        + [pl.BlockSpec((far, tile * phys_pair), lambda i: (0, place * steps + i))] * len(totals),
        out_specs=[pl.BlockSpec((far // n_outs, tile * phys_pair), lambda i: (0, i))] * n_outs,
        out_shape=[jax.ShapeDtypeStruct((far // n_outs, bonds * phys_pair), kind)] * n_outs,
        scratch_shapes=[
            pltpu.VMEM((2 * channels * phys_pair, tile // 2 * lanes), BF16),
            pltpu.VMEM((tile * phys_pair, channels * lanes), BF16),
        ],
        compiler_params=params(48),
        cost_estimate=cost(
            2 * bonds * phys_pair * right.shape[1] * (left.shape[1] + far)
            + bonds * mpo.size * lanes,
            2 * (theta.size + right.size + bonds * channels * left.shape[1])
            + 4 * far * bonds * phys_pair,
        ),
    )(theta, left, mpo, right, *totals)


def back_kernel(channels, n_parts, n_halves, *refs):
    parts = refs[:n_parts]
    mpo_ref, rights = refs[n_parts], refs[n_parts + 1 : n_parts + 1 + n_halves]
    outs, joined, ones = refs[-2 - n_halves : -2], refs[-2], refs[-1]
    lanes = rights[0].shape[1] // channels
    phys_pair = outs[0].shape[1] // lanes
    pair, step = 2 * channels, 2 * phys_pair
    pairs = outs[0].shape[0] // pair
    height = parts[0].shape[0]
    for k, part in enumerate(parts):
        joined[k * height : (k + 1) * height] = part[...]
    for right_ref, out_ref in zip(rights, outs):
        full = dot(joined[...], right_ref[...], COLS).astype(BF16)
        for i in range(pairs):
            for v in range(channels):
                ones[v * step : (v + 1) * step, i * lanes : (i + 1) * lanes] = full[
                    i * step : (i + 1) * step, v * lanes : (v + 1) * lanes
                ]
        mixed = dot(mpo_ref[...], ones[...])
        for i in range(0, pairs, 2):
            for s in range(phys_pair):
                both = [
                    mixed[s * pair : (s + 1) * pair, j * lanes : (j + 1) * lanes]
                    for j in (i, i + 1)
                ]
                out_ref[i * pair : (i + 2) * pair, s * lanes : (s + 1) * lanes] = jnp.concatenate(
                    both, axis=0
                ).astype(BF16)


def back(parts, mpo, rights, buffers, channels, phys_pair, group, groups, tile):
    columns = parts[0].shape[1]
    bonds = columns // phys_pair
    far, width = rights[0].shape
    lanes = width // channels
    steps = bonds // tile
    count = len(rights)
    before = len(parts) + 1 + count
    return pl.pallas_call(
        functools.partial(back_kernel, channels, len(parts), count),
        grid=(steps,),
        input_output_aliases={before + k: k for k in range(len(buffers))},
        in_specs=[pl.BlockSpec((p.shape[0], tile * phys_pair), lambda i: (0, i)) for p in parts]
        + [pl.BlockSpec(mpo.shape, lambda i: (0, 0), pipeline_mode=ONCE)]
        + [pl.BlockSpec((far, width), lambda i: (0, 0), pipeline_mode=ONCE)] * count
        + [ANY] * len(buffers),
        out_specs=[
            pl.BlockSpec((tile * channels, phys_pair * lanes), lambda i: (group * steps + i, 0))
        ]
        * count,
        out_shape=[jax.ShapeDtypeStruct((groups * bonds * channels, phys_pair * lanes), BF16)]
        * count,
        scratch_shapes=[
            pltpu.VMEM((far, tile * phys_pair), BF16),
            pltpu.VMEM((2 * channels * phys_pair, tile // 2 * lanes), BF16),
        ],
        compiler_params=params(48),
        cost_estimate=cost(
            count * (2 * far * width * columns + bonds * mpo.size * lanes),
            2 * count * (far * width + bonds * channels * phys_pair * lanes) + 2 * far * columns,
        ),
    )(*parts, mpo, *rights, *buffers)


def last_kernel(left_ref, back_ref, out_ref):
    out_ref[...] = dot(left_ref[...], back_ref[...]).astype(BF16)


def last(left_t, backs, chunk, n_chunks):
    columns = backs.shape[1] // n_chunks
    steps = 4
    return pl.pallas_call(
        last_kernel,
        grid=(steps,),
        in_specs=[
            pl.BlockSpec(left_t.shape, lambda i: (0, 0), pipeline_mode=ONCE),
            pl.BlockSpec((backs.shape[0], columns // steps), lambda i: (0, chunk * steps + i)),
        ],
        out_specs=pl.BlockSpec((left_t.shape[0], columns // steps), lambda i: (0, i)),
        out_shape=jax.ShapeDtypeStruct((left_t.shape[0], columns), BF16),
        compiler_params=params(48),
        cost_estimate=cost(
            2 * left_t.size * columns,
            2 * (left_t.size + left_t.shape[1] * columns + left_t.shape[0] * columns),
        ),
    )(left_t, backs)


def join_kernel(n_rows, n_parts, *refs):
    blocks, out, sems = refs[:-2], refs[-2], refs[-1]
    depth, columns = blocks[0].shape
    reach = 2 * n_rows - 1
    for phase in ("start", "wait"):
        for k, block in enumerate(blocks):
            source = lax.axis_index("row") + (k % reach - (n_rows - 1))

            @pl.when((source >= 0) & (source < n_rows))
            def _():
                target = out.at[
                    pl.ds(pl.multiple_of(source * depth, depth), depth),
                    pl.ds(k // reach * columns, columns),
                ]
                getattr(pltpu.make_async_copy(block, target, sems.at[k]), phase)()


def join(parts, n_rows):
    blocks = [block for part in parts for block in part]
    depth, columns = blocks[0].shape
    return pl.pallas_call(
        functools.partial(join_kernel, n_rows, len(parts)),
        in_specs=[ANY] * len(blocks),
        out_specs=pl.BlockSpec(memory_space=pltpu.VMEM),
        out_shape=jax.ShapeDtypeStruct((depth * n_rows, columns * len(parts)), BF16),
        scratch_shapes=[pltpu.SemaphoreType.DMA((len(blocks),))],
        compiler_params=params(),
        cost_estimate=cost(0, 4 * depth * n_rows * columns * len(parts)),
    )(*blocks)


def after(arrays, *deps):
    return lax.optimization_barrier((arrays, deps))[0]


def gather_round(pair, t, n_rows):
    up = lax.ppermute(pair[0], "row", [(r, r + 1) for r in range(t - 1, n_rows - 1)])
    down = lax.ppermute(pair[1], "row", [(r, r - 1) for r in range(1, n_rows - t + 1)])
    return up, down


def row_block(term, distance, n_rows):
    height = term.shape[0] // n_rows
    block = lax.rem(lax.axis_index("row") + distance, n_rows)
    return lax.dynamic_slice_in_dim(term, block * height, height)


def scatter_inputs(term, pair, t, n_rows):
    up, down = row_block(term, n_rows - t, n_rows), row_block(term, t, n_rows)
    if pair is not None:
        up, down = add(up, pair[0]), add(down, pair[1])
    return lax.optimization_barrier((up, down))


def scatter_round(pair, t, n_rows):
    up = lax.ppermute(pair[0], "row", [(r, r + 1) for r in range(t)])
    down = lax.ppermute(pair[1], "row", [(n_rows - 1 - r, n_rows - 2 - r) for r in range(t)])
    return up, down


def add(x, y):
    return (x.astype(F32) + y.astype(F32)).astype(BF16)


def swapped(block, axis):
    return lax.ppermute(block, axis, [(0, 1), (1, 0)])


def scattered_along(both):
    height = both.shape[0] // 2
    return add(both[:height], swapped(both[height:], "chan"))


def shards(theta, left_env, right_env, mpo_left, mpo_right):
    bonds, channels, depth = left_env.shape
    rows, phys_pair, width = theta.shape
    n_rows = lax.axis_size("row")
    scattered = lax.axis_size("col") == 2 and lax.axis_size("chan") == 2
    tile = min(32, bonds)
    lanes = min(128, width)
    halves = width // lanes
    groups = max(1, min(4, bonds // tile))
    n_chunks = 2
    per = phys_pair // n_chunks

    def mpo_pairs(*deps):
        one, two = after((mpo_left, mpo_right), *deps)
        paired = jnp.einsum("wuxs,uvyt->wstxyv", one, two, precision=lax.Precision.HIGHEST)
        mpo = paired.reshape(channels, phys_pair, phys_pair, channels).astype(BF16)
        twice = jnp.einsum("wsxv,jk->sjwvkx", mpo, jnp.eye(2, dtype=BF16))
        size = 2 * channels * phys_pair
        mpo_back = twice.reshape(size, size)
        return mpo_back.T, mpo_back

    def far_parts(*deps):
        return parted(after(right_env, *deps).transpose(1, 0, 2), lanes, scattered)

    left, left_t = ordered(left_env.transpose(1, 0, 2), tile)
    if halves == 1 or n_rows == 2:
        mpo_fore, mpo_back = mpo_pairs()
    right = far_parts() if halves == 1 else None

    theta_all, total, last_round = None, [None], [()] * n_chunks
    cuts = 2 if groups % 2 == 0 and n_rows > 2 else 1
    for h in range(halves):
        cut = theta[:, :, h * lanes : (h + 1) * lanes]
        pairs, blocks, fresh = [], [], []

        def ahead(*deps):
            return fore(
                after(theta_all, *deps, *fresh), left, mpo_fore, right[h - 1], total[0], channels,
                len(fresh), cuts, F32, tile,
            )

        for c in range(n_chunks):
            piece = cut[:, c * per : (c + 1) * per].reshape(rows, per * lanes)
            pairs.append(after((piece, piece), *last_round[c]))
            blocks.append([piece])
        for t in range(1, n_rows):
            came = list(pairs)
            if (h, t) == (0, 2):
                pairs[0] = after(pairs[0], left, left_t)
                if halves > 1:
                    mpo_fore, mpo_back = mpo_pairs(*pairs)
            if (h, t) == (0, 3) and halves > 1:
                pairs[0] = after(pairs[0], mpo_fore, mpo_back)
            if (h, t) == (1, 2):
                pairs = [after(pair, right, theta_all) for pair in pairs]
            if h > 0 and t > 2 and len(fresh) < cuts:
                fresh += ahead(*sent)
                pairs = [after(pair, fresh[-1]) for pair in pairs]
            sent = came
            for c in range(n_chunks):
                pairs[c] = gather_round(pairs[c], t, n_rows)
                blocks[c] = [pairs[c][0]] + blocks[c] + [pairs[c][1]]
        while h > 0 and len(fresh) < cuts:
            fresh += ahead(*sent)
        total = fresh or total
        last_round = pairs
        if h == 0 and halves > 1:
            right = far_parts(*pairs)
        theta_all = join(after(blocks, *fresh), n_rows)

    def forward(g, *deps):
        here = g * len(total) // groups
        return fore(
            after(theta_all, *deps), left, mpo_fore, right[-1], total[here], channels, g, groups,
            BF16, tile, g % (groups // len(total)), 2 if scattered else 1,
        )

    def backward(g, backs, *deps):
        parts = after(everyone[g], *deps)
        return back(parts, mpo_back, right, backs, channels, phys_pair, g, groups, tile)

    terms, near, own, far, everyone, backs = [], [], [], [], [], []
    step = 0
    while len(everyone) < groups or step < 2 * groups:
        g = step - groups
        waits = []
        if scattered:
            for lag, done in ((2, near), (3, own), (4, far)):
                waits += done[step - lag : step - lag + 1] if step >= lag else []
                waits += done[:1] if step == lag - 1 else []
        if step < groups:
            terms.append(forward(step, *waits))
            out = terms[-1][0]
        elif 0 <= g < len(everyone):
            backs = backward(g, backs, *waits)
            out = backs[-1]
        step += 1
        if not scattered:
            if step <= groups:
                own.append(lax.psum_scatter(out, ("col", "chan"), scatter_dimension=0, tiled=True))
                everyone.append([lax.all_gather(own[-1], ("col", "chan"), axis=0, tiled=True)])
            continue
        if len(everyone) < len(far):
            across = after(far[len(everyone)], out)
            pair = [own[len(everyone)], across]
            everyone.append(pair + [swapped(x, "col") for x in pair])
        if len(far) < len(own):
            far.append(swapped(after(own[len(far)], out), "chan"))
        if len(own) < len(near):
            own.append(scattered_along(after(near[len(own)], out)))
        if len(near) < len(terms):
            mine, other = terms[len(near)]
            near.append(add(mine, swapped(other, "col")))
        if step == 1:
            own.append(scattered_along(near[0]))
    for g in range(step - groups, groups):
        backs = backward(g, backs)

    terms, rounds = [], []

    def advance(i, *deps):
        t = len(rounds[i]) + 1
        if t < n_rows:
            pair = after(rounds[i][-1], *deps) if t > 1 else None
            ready = scatter_inputs(terms[i], pair, t, n_rows)
            rounds[i].append(scatter_round(ready, t, n_rows))
            return list(ready)

    def come(i, t):
        return list(rounds[i][min(t, len(rounds[i])) - 1])

    for i in range(halves * n_chunks):
        waits = sent + terms[-1:] if i > 0 else []
        waits += come(i - 2, 1) if i > 1 else []
        waits += come(i - 3, 2) if i > 2 else []
        terms.append(last(left_t, after(backs[i // n_chunks], *waits), i % n_chunks, n_chunks))
        rounds.append([])
        for j in range(i + 1):
            sent = advance(j, terms[-1])
    products = []
    for i in range(len(terms)):
        while len(rounds[i]) < n_rows - 1:
            advance(i)
        total = row_block(terms[i], 0, n_rows).astype(F32)
        for x in rounds[i][-1]:
            total = total + x.astype(F32)
        products.append(total.astype(BF16).reshape(rows, per, lanes))
    products = [
        jnp.concatenate(products[h * n_chunks : (h + 1) * n_chunks], axis=1) for h in range(halves)
    ]
    return jnp.concatenate(own, axis=1), jnp.concatenate(products, axis=2)


def solution(mesh):
    in_specs = (
        P(("grp", "row"), None, ("col", "chan")),
        P(("grp", "row"), None, None),
        P("grp", None, ("col", "chan")),
        P(),
        P(),
    )
    out_specs = (P(("grp", "col", "chan"), "row"), P(("grp", "row"), None, ("col", "chan")))
    return jax.shard_map(shards, mesh=mesh, in_specs=in_specs, out_specs=out_specs, check_vma=False)
```
